32 devices in a mesh: dp: 2 (over core), blk: 16 (over z, y, x).
Axes of the slice: x: 2, y: 2, z: 4, core: 2. Of those that a mesh axis runs over, the one named last changes fastest.
Arguments:
- inputs: bfloat16 [4, 1024, 1024], P('dp', 'blk'), may hold values from -6 to 6
- segments: int32 [4, 1024], P('dp', 'blk'), may hold values from 0 to 7, as said below
- pad_mask: int32 [4, 1024], P('dp', 'blk'), may hold values from 0 to 1, as said below
- timesteps: int32 [4, 8], P('dp'), may hold values from 0 to 4999
- w_qkv: bfloat16 [1024, 3072], P(('dp', 'blk')), may hold values from -0.1875 to 0.1875
- bias_query: bfloat16 [1024], P(('dp', 'blk')), may hold values from -3 to 3
- bias_value: bfloat16 [1024], P(('dp', 'blk')), may hold values from -3 to 3
- w_attn_out: bfloat16 [1024, 1024], P(('dp', 'blk')), may hold values from -1.5 to 1.5
- bias_attn_out: bfloat16 [1024], P(('dp', 'blk')), may hold values from -3 to 3
- ln1_gain: bfloat16 [1024], P(('dp', 'blk')), may hold values from 0.25 to 1.75
- ln1_shift: bfloat16 [1024], P(('dp', 'blk')), may hold values from -3 to 3
- w_ffn_in: bfloat16 [1024, 4096], P(('dp', 'blk')), may hold values from -0.1875 to 0.1875
- bias_ffn_in: bfloat16 [4096], P(('dp', 'blk')), may hold values from -3 to 3
- w_ffn_out: bfloat16 [4096, 1024], P(('dp', 'blk')), may hold values from -0.09375 to 0.09375
- bias_ffn_out: bfloat16 [1024], P(('dp', 'blk')), may hold values from -3 to 3
- ln2_gain: bfloat16 [1024], P(('dp', 'blk')), may hold values from 0.25 to 1.75
- ln2_shift: bfloat16 [1024], P(('dp', 'blk')), may hold values from -3 to 3
- cotangent: bfloat16 [4, 1024, 1024], P('dp', 'blk'), may hold values from -6 to 6
Outputs:
- outputs: bfloat16 [4, 1024, 1024], P('dp', 'blk')
- input_grad: bfloat16 [4, 1024, 1024], P('dp', 'blk')
- w_qkv_grad: float32 [1024, 3072], P(('dp', 'blk'))
- bias_query_grad: float32 [1024], P(('dp', 'blk'))
- bias_value_grad: float32 [1024], P(('dp', 'blk'))
- w_attn_out_grad: float32 [1024, 1024], P(('dp', 'blk'))
- bias_attn_out_grad: float32 [1024], P(('dp', 'blk'))
- ln1_gain_grad: float32 [1024], P(('dp', 'blk'))
- ln1_shift_grad: float32 [1024], P(('dp', 'blk'))
- w_ffn_in_grad: float32 [1024, 4096], P(('dp', 'blk'))
- bias_ffn_in_grad: float32 [4096], P(('dp', 'blk'))
- w_ffn_out_grad: float32 [4096, 1024], P(('dp', 'blk'))
- bias_ffn_out_grad: float32 [1024], P(('dp', 'blk'))
- ln2_gain_grad: float32 [1024], P(('dp', 'blk'))
- ln2_shift_grad: float32 [1024], P(('dp', 'blk'))
The draws below stay inside these ranges and needn't reach their ends.
Inputs may be any that keep to these rules, and one draw needn't show every extreme that they name: `segments`: segment ids count the items of a row from 0 and never fall. Among the 2 rows on each index of dp, exactly one holds two items: the first of 960 positions, the second of the last 64. Every other row holds items that start at multiples of 128 and are 128 or 512 positions long. The first row of all that is not a two-item row holds only items of 128 positions. `pad_mask`: each item ends in a run of padding no longer than a quarter of its length (for the first item of a two-item row, than 16); every item has real tokens.
All inputs are finite; a program needn't handle non-finite values.
Results may differ from the reference program's by a relative error of at most 0.023.
Values may be sent and summed in bfloat16 or wider, within the bound.
A program may use at most 192 MiB of HBM per device.

```python
import math
import jax
import jax.numpy as jnp
from jax import lax

D = 1024
HEADS = 16
HEAD = 64
FF = 4096
TOK = 64
SEQS_DEV = 2
ITEM_S = 128
ITEM_L = 512
TSTEPS = 5000
ROWS = 4
SEQ = 1024
NSEG = 8


def item_layout(key):
    block_count = SEQ // ITEM_S
    per_group = ITEM_L // ITEM_S
    group_count = SEQ // ITEM_L
    key_large, key_whole, key_tail = jax.random.split(key, 3)
    large = jax.random.randint(key_large, (ROWS, group_count), 0, 2)
    chosen = jax.random.randint(key_whole, (ROWS // SEQS_DEV, 1), 0, SEQS_DEV)
    whole = ((jnp.arange(ROWS) % SEQS_DEV).reshape(ROWS // SEQS_DEV, SEQS_DEV) == chosen).reshape(ROWS)
    first_parted = jnp.where(whole[0], 1, 0)
    all_short = jnp.arange(ROWS) == first_parted
    large = jnp.where(all_short[:, None], 0, large)
    blocks = jnp.arange(block_count)
    large_block = large[:, blocks // per_group]
    starts = jnp.where((blocks % per_group == 0)[None, :], 1, 1 - large_block)
    seg_block = jnp.cumsum(starts, axis=1) - 1
    item_len = jnp.where(large_block == 1, ITEM_L, ITEM_S)
    first_block = jnp.where(large_block == 1, blocks // per_group * per_group, blocks)
    tail_draw = jax.random.randint(key_tail, (ROWS, block_count), 0, 1 << 20)
    tail_raw = jnp.take_along_axis(tail_draw, first_block, axis=1)
    tail_len = tail_raw % (item_len // 4 + 1)
    positions = jnp.arange(SEQ)[None, :]
    seg_pos = jnp.repeat(seg_block, ITEM_S, axis=1)
    len_pos = jnp.repeat(item_len, ITEM_S, axis=1)
    first_pos = jnp.repeat(first_block, ITEM_S, axis=1) * ITEM_S
    tail_pos = jnp.repeat(tail_len, ITEM_S, axis=1)
    real = positions - first_pos < len_pos - tail_pos
    half_item = ITEM_S // 2
    wide_end = SEQ - half_item
    tail_wide = tail_draw[:, 0] % (TOK // 4 + 1)
    tail_last = tail_draw[:, 1] % (half_item // 4 + 1)
    seg_whole = (positions >= wide_end).astype(jnp.int32)
    real_whole = jnp.where(positions < wide_end, positions < wide_end - tail_wide[:, None], positions < SEQ - tail_last[:, None])
    seg_pos = jnp.where(whole[:, None], seg_whole, seg_pos)
    real = jnp.where(whole[:, None], real_whole, real)
    return (seg_pos.astype(jnp.int32), real.astype(jnp.int32))


def draw_segments(key, part):
    shared = item_layout(key)
    return shared[0]


def draw_pad_mask(key, part):
    shared = item_layout(key)
    return shared[1]


def place_ends(entries, own_key, smallest, high):
    longest = entries.shape.index(max(entries.shape))
    spots = []
    for shift in (0, 1):
        where = [jax.random.randint(jax.random.fold_in(own_key, axis), (), 0, length) for axis, length in enumerate(entries.shape)]
        where[longest] = (where[longest] + shift) % entries.shape[longest]
        spots.append(tuple(where))
    return entries.at[spots[0]].set(smallest).at[spots[1]].set(high)


def level_of(own_key, shape, shards, smallest, high):
    level = 1.0
    for dim, shards_of in shards:
        draws = jax.random.uniform(jax.random.fold_in(jax.random.fold_in(own_key, 6), dim), (shards_of,), jnp.float32, smallest / len(shards), high / len(shards))
        level = level * jnp.repeat(jnp.exp(draws), shape[dim] // shards_of).reshape((-1,) + (1,) * (len(shape) - 1 - dim))
    return level


def gaussian(rng, dims, scale, bound, cuts=(), kind=jnp.bfloat16):
    factor_of = level_of(rng, dims, cuts, -0.22, 0.18) if cuts else 1.0
    entries = jax.random.normal(rng, dims, jnp.float32) * scale * factor_of
    return jnp.minimum(jnp.maximum(entries, -bound), bound).astype(kind)


def setup_inputs(seed: int = 0) -> dict:
    seeds = jax.random.split(jax.random.key(seed), 19)
    return {
        "inputs": gaussian(seeds[0], (ROWS, SEQ, D), 1.0, 6.0, ((0, 2), (1, 16))),
        "segments": draw_segments(jax.random.fold_in(seeds[18], 71), 0),
        "pad_mask": draw_pad_mask(jax.random.fold_in(seeds[18], 71), 0),
        "timesteps": place_ends(jax.random.randint(seeds[3], (ROWS, NSEG), 0, TSTEPS), jax.random.fold_in(seeds[3], 1), 0, TSTEPS - 1).astype(jnp.int32),
        "w_qkv": gaussian(seeds[4], (D, 3 * D), D ** -0.5, 0.1875, ((0, 32),)),
        "bias_query": gaussian(seeds[5], (D,), 0.5, 3.0, ((0, 32),)),
        "bias_value": gaussian(seeds[6], (D,), 0.5, 3.0, ((0, 32),)),
        "w_attn_out": gaussian(seeds[7], (D, D), (D // 64) ** -0.5, 1.5, ((0, 32),)),
        "bias_attn_out": gaussian(seeds[8], (D,), 0.5, 3.0, ((0, 32),)),
        "ln1_gain": jnp.clip(1.0 + 0.15 * jax.random.normal(seeds[9], (D,), jnp.float32), 0.25, 1.75).astype(jnp.bfloat16),
        "ln1_shift": gaussian(seeds[10], (D,), 0.5, 3.0, ((0, 32),)),
        "w_ffn_in": gaussian(seeds[11], (D, FF), D ** -0.5, 0.1875, ((0, 32),)),
        "bias_ffn_in": gaussian(seeds[12], (FF,), 0.5, 3.0, ((0, 32),)),
        "w_ffn_out": gaussian(seeds[13], (FF, D), FF ** -0.5, 0.09375, ((0, 32),)),
        "bias_ffn_out": gaussian(seeds[14], (D,), 0.5, 3.0, ((0, 32),)),
        "ln2_gain": jnp.clip(1.0 + 0.15 * jax.random.normal(seeds[15], (D,), jnp.float32), 0.25, 1.75).astype(jnp.bfloat16),
        "ln2_shift": gaussian(seeds[16], (D,), 0.5, 3.0, ((0, 32),)),
        "cotangent": gaussian(seeds[17], (ROWS, SEQ, D), 1.0, 6.0, ((0, 2), (1, 16))),
    }


EPSILON = 1e-05
NEGATIVE = -1e+30
HIGH = lax.Precision.HIGHEST

@jax.custom_vjp
def low(v):
    return lax.optimization_barrier(v.astype(jnp.bfloat16)).astype(jnp.float32)

@jax.custom_vjp
def low_back(v):
    return v

def low_keep(v):
    return (low(v), None)

def low_pass(kept, grad):
    return (grad,)

def back_keep(v):
    return (v, None)

def back_low(kept, grad):
    return (low(grad),)
low.defvjp(low_keep, low_pass)
low_back.defvjp(back_keep, back_low)

def time_features(timesteps, segments, model_width):
    item_count = timesteps.shape[1]
    numbers = jnp.arange(item_count, dtype=jnp.int32)
    picked = lax.optimization_barrier(jnp.sum(jnp.where(segments[:, :, None] == numbers[None, None, :], timesteps[:, None, :], 0), axis=-1))
    half_width = model_width // 2
    frequency = jnp.exp(jnp.arange(half_width, dtype=jnp.float32) * (-math.log(10000.0) / half_width))
    angles = picked.astype(jnp.float32)[..., None] * (100.0 / TSTEPS) * frequency
    return jnp.concatenate([jnp.sin(angles), jnp.cos(angles)], axis=-1)

def layer_norm(hidden, gain, shift):
    centered = hidden - lax.optimization_barrier(jnp.mean(hidden, axis=-1, keepdims=True))
    variance = lax.optimization_barrier(jnp.mean(centered * centered, axis=-1, keepdims=True))
    return centered * lax.rsqrt(variance + EPSILON) * gain + shift

def matmul(left, right):
    return jnp.dot(left, right, precision=HIGH)

def attend_block(item, keys_row, values_row, code_row):
    query_block, seg_block = item
    scores = jnp.einsum('qhe,khe->hqk', query_block, keys_row, precision=HIGH) * HEAD ** (-0.5)
    scores = low_back(scores)
    valid = seg_block[None, :, None] == code_row[None, None, :]
    probs = jax.nn.softmax(jnp.where(valid, scores, NEGATIVE), axis=-1)
    probs = low(probs)
    return jnp.einsum('hqk,khe->qhe', probs, values_row, precision=HIGH)

def attend_row(queries, keys_row, values_row, seg_row, code_row):
    block_rows = 512 if SEQ % 512 == 0 else SEQ
    blocks = SEQ // block_rows
    query_heads = queries.reshape(blocks, block_rows, HEADS, HEAD)
    key_heads = keys_row.reshape(SEQ, HEADS, HEAD)
    value_heads = values_row.reshape(SEQ, HEADS, HEAD)
    block_fn = jax.checkpoint(attend_block)
    result = lax.map(lambda item: block_fn(item, key_heads, value_heads, code_row), (query_heads, seg_row.reshape(blocks, block_rows)))
    return result.reshape(SEQ, D)

def layer_row(item, params):
    row_in, seg_row, code_row, emb_row = item
    qkv_weight, query_bias, value_bias, out_weight, out_bias, gain_one, shift_one, in_weight, in_bias, down_weight, down_bias, gain_two, shift_two = params
    start_res = row_in + emb_row
    start_low = low(start_res)
    projected = matmul(start_low, qkv_weight)
    queries = low(low_back(projected[:, :D] + query_bias))
    keys_row = low(low_back(projected[:, D:2 * D]))
    values_row = low(low_back(projected[:, 2 * D:] + value_bias))
    attended = attend_row(queries, keys_row, values_row, seg_row, code_row)
    attended_low = low(low_back(attended))
    attn_branch = low_back(matmul(attended_low, out_weight) + out_bias)
    after_attn = layer_norm(start_res + attn_branch, gain_one, shift_one)
    pre_act = low_back(matmul(low(after_attn), in_weight) + in_bias)
    activated = low(jax.nn.gelu(pre_act, approximate=False))
    branch = low_back(matmul(activated, down_weight) + down_bias)
    return layer_norm(after_attn + branch, gain_two, shift_two)

def reference(inputs, segments, pad_mask, timesteps, w_qkv, bias_query, bias_value, w_attn_out, bias_attn_out, ln1_gain, ln1_shift, w_ffn_in, bias_ffn_in, w_ffn_out, bias_ffn_out, ln2_gain, ln2_shift, cotangent):
    embedded = time_features(timesteps, segments, D)
    codes = jnp.where(pad_mask == 1, segments, -1)
    params = tuple((param.astype(jnp.float32) for param in (w_qkv, bias_query, bias_value, w_attn_out, bias_attn_out, ln1_gain, ln1_shift, w_ffn_in, bias_ffn_in, w_ffn_out, bias_ffn_out, ln2_gain, ln2_shift)))
    row_fn = jax.checkpoint(layer_row)

    def forward(start, weights):
        return lax.map(lambda item: row_fn(item, weights), (start, segments, codes, embedded))
    outputs, pullback = jax.vjp(forward, inputs.astype(jnp.float32), params)
    input_grad, grads = pullback(cotangent.astype(jnp.float32))
    return (outputs.astype(jnp.bfloat16), input_grad.astype(jnp.bfloat16), grads[0], grads[1], grads[2], grads[3], grads[4], grads[5], grads[6], grads[7], grads[8], grads[9], grads[10], grads[11], grads[12])
```

```python
import functools
import math

import jax
import jax.numpy as jnp
from jax import lax
from jax.experimental import pallas as pl
from jax.experimental.pallas import tpu as pltpu
from jax.sharding import PartitionSpec as P

HEADS = 16
HEAD = 64
TSTEPS = 5000


EPSILON = 1e-05
NEGATIVE = -1e30


def time_features(timesteps, segments, model_width):
    item_count = timesteps.shape[1]
    numbers = jnp.arange(item_count, dtype=jnp.int32)
    picked = jnp.sum(
        jnp.where(segments[:, :, None] == numbers[None, None, :], timesteps[:, None, :], 0), axis=-1
    )
    half_width = model_width // 2
    frequency = jnp.exp(
        jnp.arange(half_width, dtype=jnp.float32) * (-math.log(10000.0) / half_width)
    )
    angles = picked.astype(jnp.float32)[..., None] * (100.0 / TSTEPS) * frequency
    return jnp.concatenate([jnp.sin(angles), jnp.cos(angles)], axis=-1)


def normalize(hidden):
    centered = hidden - jnp.mean(hidden, axis=-1, keepdims=True)
    inverse = lax.rsqrt(jnp.mean(centered * centered, axis=-1, keepdims=True) + EPSILON)
    return (centered * inverse, inverse)


def norm_backward(upstream, normed, inverse, gain):
    scaled = upstream * gain
    return inverse * (
        scaled
        - jnp.mean(scaled, axis=-1, keepdims=True)
        - normed * jnp.mean(scaled * normed, axis=-1, keepdims=True)
    )


def exact_gelu(values):
    return jax.nn.gelu(values, approximate=False)


def local(
    inputs,
    segments,
    pad_mask,
    timesteps,
    w_qkv,
    bias_query,
    bias_value,
    w_attn_out,
    bias_attn_out,
    ln1_gain,
    ln1_shift,
    w_ffn_in,
    bias_ffn_in,
    w_ffn_out,
    bias_ffn_out,
    ln2_gain,
    ln2_shift,
    cotangent,
):
    row_count, tok_count, model_width = inputs.shape
    flat_count = row_count * tok_count
    head_count = HEADS
    head_dim = HEAD
    scale = HEAD ** (-0.5)
    bf16 = jnp.bfloat16
    single = jnp.float32
    attn_full = (
        lax.all_gather(w_qkv, ("dp", "blk"), axis=0, tiled=True),
        lax.all_gather(bias_query, ("dp", "blk"), axis=0, tiled=True),
        lax.all_gather(bias_value, ("dp", "blk"), axis=0, tiled=True),
        lax.all_gather(w_attn_out, ("dp", "blk"), axis=0, tiled=True),
        lax.all_gather(bias_attn_out, ("dp", "blk"), axis=0, tiled=True),
        lax.all_gather(ln1_gain, ("dp", "blk"), axis=0, tiled=True),
        lax.all_gather(ln1_shift, ("dp", "blk"), axis=0, tiled=True),
    )
    qkv_weight, query_bias, value_bias, out_weight, out_bias, gain_one, shift_one = attn_full
    embedded = time_features(timesteps, segments, model_width)
    start_flat = (inputs.astype(single) + embedded).reshape(flat_count, model_width)
    start_low = start_flat.astype(bf16)
    projected = jnp.dot(start_low, qkv_weight, preferred_element_type=single)
    query_send = (
        (projected[:, :model_width] + query_bias.astype(single))
        .astype(bf16)
        .reshape(row_count, tok_count, model_width)
    )
    key_send = (
        projected[:, model_width : 2 * model_width]
        .astype(bf16)
        .reshape(row_count, tok_count, model_width)
    )
    value_send = (
        (projected[:, 2 * model_width :] + value_bias.astype(single))
        .astype(bf16)
        .reshape(row_count, tok_count, model_width)
    )
    query_heads = query_send.reshape(row_count, tok_count, head_count, head_dim)
    key_heads = key_send.reshape(row_count, tok_count, head_count, head_dim)
    value_heads = value_send.reshape(row_count, tok_count, head_count, head_dim)
    codes = jnp.where(pad_mask == 1, segments, -1)
    code_float = codes.astype(single)
    seg_float = segments.astype(single)
    code_send = codes.astype(bf16)
    seg_send = segments.astype(bf16)

    def split_heads(piece):
        return piece.reshape(piece.shape[0], piece.shape[1], head_count, head_dim)

    piece = (
        lax.all_gather(key_send, "blk", axis=1, tiled=True),
        lax.all_gather(value_send, "blk", axis=1, tiled=True),
        lax.all_gather(code_send, "blk", axis=1, tiled=True),
    )
    run_max = jnp.full((row_count, tok_count, head_count), NEGATIVE, single)
    piece_keys = split_heads(piece[0])
    piece_values = split_heads(piece[1])
    scores = (
        jnp.einsum("rqhe,rkhe->rqhk", query_heads, piece_keys, preferred_element_type=single)
        * scale
    )
    valid = seg_float[:, :, None, None] == piece[2].astype(single)[:, None, None, :]
    masked = jnp.where(valid, scores, NEGATIVE)
    new_max = jnp.maximum(run_max, jnp.max(masked, axis=-1))
    weights = jnp.where(valid, jnp.exp(masked - new_max[..., None]), 0.0)
    run_sum = jnp.sum(weights, axis=-1)
    run_acc = jnp.einsum(
        "rqhk,rkhe->rqhe", weights.astype(bf16), piece_values, preferred_element_type=single
    )
    run_max, run_sum, run_acc = (new_max, run_sum, run_acc)
    log_total = run_max + jnp.log(run_sum)
    attended = run_acc / run_sum[..., None]
    attended_low = attended.reshape(flat_count, model_width).astype(bf16)
    attn_branch = jnp.dot(
        attended_low, out_weight, preferred_element_type=single
    ) + out_bias.astype(single)
    normed_one, inverse_one = normalize(start_flat + attn_branch)
    gain_one_f = gain_one.astype(single)
    after_attn = normed_one * gain_one_f + shift_one.astype(single)
    ffn_full = (
        lax.all_gather(w_ffn_in, ("dp", "blk"), axis=0, tiled=True),
        lax.all_gather(bias_ffn_in, ("dp", "blk"), axis=0, tiled=True),
        lax.all_gather(w_ffn_out, ("dp", "blk"), axis=0, tiled=True),
        lax.all_gather(bias_ffn_out, ("dp", "blk"), axis=0, tiled=True),
        lax.all_gather(ln2_gain, ("dp", "blk"), axis=0, tiled=True),
        lax.all_gather(ln2_shift, ("dp", "blk"), axis=0, tiled=True),
    )
    in_weight, in_bias, down_weight, down_bias, gain_two, shift_two = ffn_full
    hidden_low = after_attn.astype(bf16)
    pre_act = jnp.dot(hidden_low, in_weight, preferred_element_type=single) + in_bias.astype(single)
    activated, gelu_pull = jax.vjp(exact_gelu, pre_act)
    activated_low = activated.astype(bf16)
    branch = jnp.dot(activated_low, down_weight, preferred_element_type=single) + down_bias.astype(
        single
    )
    normed_two, inverse_two = normalize(after_attn + branch)
    gain_two_f = gain_two.astype(single)
    outputs = (
        (normed_two * gain_two_f + shift_two.astype(single))
        .astype(bf16)
        .reshape(row_count, tok_count, model_width)
    )
    ffn_back = (
        lax.all_gather(w_ffn_in, ("dp", "blk"), axis=0, tiled=True),
        lax.all_gather(w_ffn_out, ("dp", "blk"), axis=0, tiled=True),
    )
    in_weight_back, down_weight_back = ffn_back
    upstream = cotangent.astype(single).reshape(flat_count, model_width)
    gain_two_grad = jnp.sum(upstream * normed_two, axis=0)
    shift_two_grad = jnp.sum(upstream, axis=0)
    second_grad = norm_backward(upstream, normed_two, inverse_two, gain_two_f)
    branch_grad = second_grad.astype(bf16)
    down_weight_grad = jnp.einsum(
        "tf,td->fd", activated_low, branch_grad, preferred_element_type=single
    )
    down_bias_grad = jnp.sum(branch_grad.astype(single), axis=0)
    act_grad = jnp.einsum("td,fd->tf", branch_grad, down_weight_back, preferred_element_type=single)
    pre_grad = gelu_pull(act_grad)[0].astype(bf16)
    in_weight_grad = jnp.einsum("td,tf->df", hidden_low, pre_grad, preferred_element_type=single)
    in_bias_grad = jnp.sum(pre_grad.astype(single), axis=0)
    hidden_grad = second_grad + jnp.einsum(
        "tf,df->td", pre_grad, in_weight_back, preferred_element_type=single
    )
    gain_one_grad = jnp.sum(hidden_grad * normed_one, axis=0)
    shift_one_grad = jnp.sum(hidden_grad, axis=0)
    first_grad = norm_backward(hidden_grad, normed_one, inverse_one, gain_one_f)
    ffn_grads = (
        lax.psum_scatter(in_weight_grad, ("dp", "blk"), scatter_dimension=0, tiled=True),
        lax.psum_scatter(in_bias_grad, ("dp", "blk"), scatter_dimension=0, tiled=True),
        lax.psum_scatter(down_weight_grad, ("dp", "blk"), scatter_dimension=0, tiled=True),
        lax.psum_scatter(down_bias_grad, ("dp", "blk"), scatter_dimension=0, tiled=True),
        lax.psum_scatter(gain_two_grad, ("dp", "blk"), scatter_dimension=0, tiled=True),
        lax.psum_scatter(shift_two_grad, ("dp", "blk"), scatter_dimension=0, tiled=True),
    )
    attn_back = (
        lax.all_gather(w_qkv, ("dp", "blk"), axis=0, tiled=True),
        lax.all_gather(w_attn_out, ("dp", "blk"), axis=0, tiled=True),
    )
    qkv_weight_back, out_weight_back = attn_back
    attn_grad_low = first_grad.astype(bf16)
    out_weight_grad = jnp.einsum(
        "td,te->de", attended_low, attn_grad_low, preferred_element_type=single
    )
    out_bias_grad = jnp.sum(attn_grad_low.astype(single), axis=0)
    attended_grad = jnp.einsum(
        "te,de->td", attn_grad_low, out_weight_back, preferred_element_type=single
    ).astype(bf16)
    grad_send = attended_grad.reshape(row_count, tok_count, model_width)
    grad_heads = grad_send.reshape(row_count, tok_count, head_count, head_dim)
    residue = jnp.sum(grad_heads.astype(single) * attended, axis=-1)
    stats_full = (
        lax.all_gather(log_total, "blk", axis=1, tiled=True),
        lax.all_gather(residue, "blk", axis=1, tiled=True),
    )
    log_full, residue_full = stats_full
    piece = (
        lax.all_gather(key_send, "blk", axis=1, tiled=True),
        lax.all_gather(value_send, "blk", axis=1, tiled=True),
        lax.all_gather(code_send, "blk", axis=1, tiled=True),
    )
    piece_keys = split_heads(piece[0])
    piece_values = split_heads(piece[1])
    scores = (
        jnp.einsum("rqhe,rkhe->rqhk", query_heads, piece_keys, preferred_element_type=single)
        * scale
    )
    valid = seg_float[:, :, None, None] == piece[2].astype(single)[:, None, None, :]
    probs = jnp.exp(jnp.where(valid, scores - log_total[..., None], NEGATIVE))
    prob_grad = jnp.einsum(
        "rqhe,rkhe->rqhk", grad_heads, piece_values, preferred_element_type=single
    )
    score_grad = (probs * (prob_grad - residue[..., None])).astype(bf16)
    query_grad = (
        jnp.einsum("rqhk,rkhe->rqhe", score_grad, piece_keys, preferred_element_type=single) * scale
    )
    piece = (
        lax.all_gather(query_send, "blk", axis=1, tiled=True),
        lax.all_gather(grad_send, "blk", axis=1, tiled=True),
        lax.all_gather(seg_send, "blk", axis=1, tiled=True),
    )
    piece_queries = split_heads(piece[0])
    piece_grads = split_heads(piece[1])
    scores = (
        jnp.einsum("rqhe,rkhe->rqhk", piece_queries, key_heads, preferred_element_type=single)
        * scale
    )
    valid = piece[2].astype(single)[:, :, None, None] == code_float[:, None, None, :]
    probs = jnp.exp(jnp.where(valid, scores - log_full[..., None], NEGATIVE))
    value_acc = jnp.einsum(
        "rqhk,rqhe->rkhe", probs.astype(bf16), piece_grads, preferred_element_type=single
    )
    prob_grad = jnp.einsum(
        "rqhe,rkhe->rqhk", piece_grads, value_heads, preferred_element_type=single
    )
    score_grad = (probs * (prob_grad - residue_full[..., None])).astype(bf16)
    key_acc = (
        jnp.einsum("rqhk,rqhe->rkhe", score_grad, piece_queries, preferred_element_type=single)
        * scale
    )
    query_low = query_grad.astype(bf16).reshape(flat_count, model_width)
    key_low = key_acc.astype(bf16).reshape(flat_count, model_width)
    value_low = value_acc.astype(bf16).reshape(flat_count, model_width)
    qkv_grad = jnp.concatenate([query_low, key_low, value_low], axis=1)
    qkv_weight_grad = jnp.einsum("td,tc->dc", start_low, qkv_grad, preferred_element_type=single)
    query_bias_grad = jnp.sum(query_low.astype(single), axis=0)
    value_bias_grad = jnp.sum(value_low.astype(single), axis=0)
    input_grad = (
        first_grad
        + jnp.einsum("tc,dc->td", qkv_grad, qkv_weight_back, preferred_element_type=single)
    ).astype(bf16)
    input_grad = input_grad.reshape(row_count, tok_count, model_width)
    attn_grads = (
        lax.psum_scatter(qkv_weight_grad, ("dp", "blk"), scatter_dimension=0, tiled=True),
        lax.psum_scatter(query_bias_grad, ("dp", "blk"), scatter_dimension=0, tiled=True),
        lax.psum_scatter(value_bias_grad, ("dp", "blk"), scatter_dimension=0, tiled=True),
        lax.psum_scatter(out_weight_grad, ("dp", "blk"), scatter_dimension=0, tiled=True),
        lax.psum_scatter(out_bias_grad, ("dp", "blk"), scatter_dimension=0, tiled=True),
        lax.psum_scatter(gain_one_grad, ("dp", "blk"), scatter_dimension=0, tiled=True),
        lax.psum_scatter(shift_one_grad, ("dp", "blk"), scatter_dimension=0, tiled=True),
    )
    return (
        outputs,
        input_grad,
        attn_grads[0],
        attn_grads[1],
        attn_grads[2],
        attn_grads[3],
        attn_grads[4],
        attn_grads[5],
        attn_grads[6],
        ffn_grads[0],
        ffn_grads[1],
        ffn_grads[2],
        ffn_grads[3],
        ffn_grads[4],
        ffn_grads[5],
    )


MESH = pl.DeviceIdType.MESH
PLANE = 4
PLANES = 4
TILE = 256
BF16 = jnp.bfloat16
F32 = jnp.float32


def mm(left, right, left_dim=1, right_dim=0):
    return lax.dot_general(
        left, right, (((left_dim,), (right_dim,)), ((), ())), preferred_element_type=F32
    )


def wide_slice(start, size, step):
    return pl.ds(pl.multiple_of(start, step), size)


class Names:
    pass


class Labels:
    def __getattr__(self, name):
        return name


N = Labels()
SEND, RECV = 0, 1


def scratch_plan(tok, model, hidden):
    chunk = 2 * tok
    toks = PLANE * chunk
    keys = 2 * toks
    wid = model // PLANE
    units = hidden // PLANE
    rows = model // 32
    zrows = PLANE * rows
    half = PLANES * zrows
    return dict(
        xin=((chunk, model), BF16),
        cin=((chunk, model), BF16),
        tbl=((8, model), F32),
        inf_in=((2, 8, 128), F32),
        inf=((8, 8, 128), F32),
        smalls=((2, PLANES, PLANE, 16, 128), BF16),
        vec=((16, model), F32),
        ffb=((16, units), F32),
        wqkv=((model, 3 * wid), BF16),
        wo=((model, model), BF16),
        win=((model, units), BF16),
        wfo=((units, model), BF16),
        sres=((chunk, model), F32),
        slow=((toks, model), BF16),
        q=((toks, wid), BF16),
        kv=((keys, 2 * wid), BF16),
        bias=((toks, keys), F32),
        att=((toks, wid), F32),
        lse=((4, toks, 1), F32),
        attl=((toks, wid), BF16),
        attx=((chunk, model), BF16),
        n1=((chunk, model), F32),
        inv1=((chunk, 1), F32),
        aft=((chunk, model), F32),
        hid=((toks, model), BF16),
        pre=((toks, units), F32),
        act=((toks, units), BF16),
        fs=((PLANE, chunk, model), BF16),
        fr=((PLANE, chunk, model), BF16),
        own=((chunk, model), F32),
        outl=((chunk, model), BF16),
        outr=((2, tok, model), BF16),
        second=((chunk, model), F32),
        bg=((toks, model), BF16),
        pg=((toks, units), BF16),
        first=((chunk, model), F32),
        agl=((chunk, model), BF16),
        ado=((chunk, model), BF16),
        do=((toks, wid), BF16),
        dq=((toks, wid), F32),
        dk=((keys, wid), F32),
        dv=((keys, wid), F32),
        dkvs=((toks, 2 * wid), BF16),
        dkvr=((toks, 2 * wid), BF16),
        dqkv=((toks, 3 * wid), BF16),
        igl=((chunk, model), BF16),
        igr=((2, tok, model), BF16),
        gfo_s=((half, model), BF16),
        gfo_r=((half, model), BF16),
        gfo_o=((zrows, model), F32),
        gfo_zs=((4, zrows, model), BF16),
        gfo_zr=((4, zrows, model), BF16),
        gwi_s=((half, units), BF16),
        gwi_r=((half, units), BF16),
        gwi_o=((zrows, units), F32),
        gwi_zs=((4, zrows, units), BF16),
        gwi_zr=((4, zrows, units), BF16),
        gwi_p=((zrows, units), BF16),
        gwi_pr=((4, rows, units), BF16),
        gqk_s=((half, 3 * wid), BF16),
        gqk_r=((half, 3 * wid), BF16),
        gqk_o=((zrows, 3 * wid), F32),
        gqk_zs=((4, zrows, 3 * wid), BF16),
        gqk_zr=((4, zrows, 3 * wid), BF16),
        gqk_p=((zrows, 3 * wid), BF16),
        gqk_pr=((4, rows, 3 * wid), BF16),
        gwo_s=((half, model), BF16),
        gwo_r=((half, model), BF16),
        gwo_o=((half, model), F32),
        gwo_p=((half, model), BF16),
        gwo_pr=((4, PLANES, rows, model), BF16),
        gwo_zs=((4, rows, model), BF16),
        gwo_zr=((4, rows, model), BF16),
        smg=((16, model), F32),
        sma=((8, 16, 128), F32),
        smb=((16, 128), F32),
        smb_r=((4, 16, 128), F32),
    )


N_SEND = 64
N_RECV = 160


def fused(plan, tok, model, hidden, *refs):
    (x_ref, cot_ref, table_ref, small_ref, info_ref, wqkv_ref, wo_ref, win_ref, wfo_ref) = refs[:9]
    (out_ref, ig_ref, dwqkv_ref, dwo_ref, dwin_ref, dwfo_ref, sg_ref) = refs[9:16]
    s = Names()
    for name, ref in zip(plan, refs[16:]):
        setattr(s, name, ref)
    send_pool, recv_pool = refs[16 + len(plan):]

    chunk = 2 * tok
    toks = PLANE * chunk
    keys = 2 * toks
    wid = model // PLANE
    units = hidden // PLANE
    rows = model // 32
    zrows = PLANE * rows
    half = PLANES * zrows
    heads = wid // HEAD
    frows = hidden // 32

    c = lax.axis_index("dp")
    b = lax.axis_index("blk")
    z = b // PLANE
    p = b % PLANE
    y, x = p // 2, p % 2
    other = 1 - c
    plane_peers = [p, y * 2 + (1 - x), (1 - y) * 2 + x, PLANE - 1 - p]
    z_peers = [(z + k) % PLANES for k in range(PLANES)]
    z_back = [(z + PLANES - k) % PLANES for k in range(PLANES)]

    def dev(cc, zz, pp):
        return {"dp": cc, "blk": zz * PLANE + pp}

    used = ({}, {})

    def sem(kind, name):
        table = used[kind]
        if name not in table:
            table[name] = len(table)
            assert table[name] < (N_SEND, N_RECV)[kind]
        return (send_pool, recv_pool)[kind].at[table[name]]

    pending = []

    def remote(src, dst, send_name, recv_name, target):
        pltpu.make_async_remote_copy(
            src_ref=src,
            dst_ref=dst,
            send_sem=sem(SEND, send_name),
            recv_sem=sem(RECV, recv_name),
            device_id=target,
            device_id_type=MESH,
        ).start()

    def sent(ref, send_name, cond=None):
        pending.append((ref, send_name, cond))

    def flush_sent():
        for ref, send_name, cond in pending:
            def one():
                handle = sem(SEND, send_name)
                pltpu.make_async_copy(ref, ref, handle).wait()
            if cond is None:
                one()
            else:
                pl.when(cond)(one)
        pending.clear()

    def arrived(ref, recv_name):
        pltpu.make_async_copy(ref, ref, sem(RECV, recv_name)).wait()

    def maybe_local(src, dst, send_name, recv_name, target, is_self):
        send_handle = sem(SEND, send_name)
        recv_handle = sem(RECV, recv_name)

        @pl.when(is_self)
        def _():
            pltpu.make_async_copy(src, dst, recv_handle).start()

        @pl.when(jnp.logical_not(is_self))
        def _():
            pltpu.make_async_remote_copy(
                src_ref=src, dst_ref=dst, send_sem=send_handle, recv_sem=recv_handle,
                device_id=target, device_id_type=MESH,
            ).start()

        sent(src, send_name, jnp.logical_not(is_self))

    barrier = pltpu.get_barrier_semaphore()
    greeted = [dev(c, z, plane_peers[k]) for k in (1, 2, 3)]
    greeted += [dev(c, z_peers[k], p) for k in (1, 2, 3)]
    greeted += [dev(other, z_peers[k], p) for k in (0, 1, 2, 3)]
    for target in greeted:
        pl.semaphore_signal(barrier, inc=1, device_id=target, device_id_type=MESH)
    pl.semaphore_wait(barrier, len(greeted))

    home = z // 2
    slot = z % 2
    for i in range(2):
        plane_of = 2 * c + i
        is_self = jnp.logical_and(home == c, plane_of == z)
        target = dev(home, plane_of, p)
        maybe_local(x_ref.at[i], s.xin.at[wide_slice(slot * tok, tok, tok)], (N.x, i), N.x, target, is_self)
        maybe_local(info_ref.at[i], s.inf_in.at[slot], (N.i, i), N.i, target, is_self)

    table_here = home == c

    @pl.when(table_here)
    def _():
        remote(table_ref.at[slot], s.tbl, N.tbl, N.tbl, dev(other, z, p))
        s.tbl[...] = table_ref[slot]

    wrow = (c * 16 + z * 4 + p) * rows
    for t in range(3):
        pltpu.make_async_copy(
            wqkv_ref.at[:, wide_slice(t * model + p * wid, wid, wid)],
            s.wqkv.at[wide_slice(wrow, rows, rows), pl.ds(t * wid, wid)],
            sem(RECV, N.wq0),
        ).start()
    for k in (3, 1, 2):
        pp = plane_peers[k]
        for t in range(3):
            remote(
                wqkv_ref.at[:, wide_slice(t * model + pp * wid, wid, wid)],
                s.wqkv.at[wide_slice(wrow, rows, rows), pl.ds(t * wid, wid)],
                (N.wq1, k), (N.wq1, k), dev(c, z, pp),
            )
        sent(s.wqkv.at[pl.ds(0, rows)], (N.wq1, k))

    s.smalls[c, z, p] = small_ref[...]
    for k in (1, 2, 3):
        remote(small_ref, s.smalls.at[c, z, p], N.smz, (N.smz, k), dev(c, z_peers[k], p))
    sent(s.smalls.at[0, 0, pl.ds(0, 3)], N.smz)

    pltpu.make_async_copy(wo_ref, s.wo.at[wide_slice(wrow, rows, rows)], sem(RECV, N.wo0)).start()
    for k in (1, 2, 3):
        remote(wo_ref, s.wo.at[wide_slice(wrow, rows, rows)], N.woz, (N.woz, k), dev(c, z_peers[k], p))
    sent(s.wo.at[pl.ds(0, 3 * rows)], N.woz)

    arrived(s.wqkv.at[pl.ds(0, rows)], N.wq0)
    for k in (1, 2, 3):
        arrived(s.wqkv.at[pl.ds(0, rows)], (N.wq1, k))
    zrow = c * half + z * zrows
    wq_block = s.wqkv.at[wide_slice(zrow, zrows, zrows)]
    for k in (1, 2, 3):
        remote(wq_block, wq_block, N.wq2, (N.wq2, k), dev(c, z_peers[k], p))
    sent(s.wqkv.at[pl.ds(0, 3 * zrows)], N.wq2)
    remote(wq_block, wq_block, N.wq3, N.wq3, dev(other, z, p))

    arrived(s.inf_in, N.i)
    info_own = s.inf_in[0] + s.inf_in[1]
    s.inf[c * 4 + p] = info_own
    for k in (1, 2, 3):
        blk_ref = s.inf.at[c * 4 + p]
        remote(blk_ref, blk_ref, N.inf, (N.inf, k), dev(c, z, plane_peers[k]))
    sent(s.inf.at[pl.ds(0, 3)], N.inf)

    @pl.when(jnp.logical_not(table_here))
    def _():
        arrived(s.tbl, N.tbl)

    arrived(s.xin, N.x)
    items = lax.broadcasted_iota(jnp.int32, (8, chunk), 0).astype(F32)
    onehot = jnp.where(info_own[0:1, :] == items + 1.0, 1.0, 0.0)
    embedded = lax.dot_general(
        onehot, s.tbl[...], (((0,), (0,)), ((), ())), precision=lax.Precision.HIGHEST,
        preferred_element_type=F32,
    )
    start_res = s.xin[...].astype(F32) + embedded
    s.sres[...] = start_res
    prow = p * chunk
    own_rows = wide_slice(prow, chunk, chunk)
    s.slow[own_rows, :] = start_res.astype(BF16)

    def plane_gather(ref, name):
        for k in (1, 2, 3):
            block = ref.at[own_rows]
            remote(block, block, name, (name, k), dev(c, z, plane_peers[k]))
        sent(ref.at[pl.ds(0, 3 * chunk)], name)

    plane_gather(s.slow, N.slow)

    for i in range(2):
        plane_of = 2 * c + i
        is_self = jnp.logical_and(home == c, plane_of == z)
        target = dev(home, plane_of, p)
        maybe_local(cot_ref.at[i], s.cin.at[wide_slice(slot * tok, tok, tok)], (N.c, i), N.c, target, is_self)
    for g in range(8):
        pltpu.make_async_copy(
            win_ref.at[:, wide_slice(g * 4 * frows + p * frows, frows, frows)],
            s.win.at[wide_slice(wrow, rows, rows), pl.ds(g * frows, frows)],
            sem(RECV, N.wi0),
        ).start()
    for k in (3, 1, 2):
        pp = plane_peers[k]
        for g in range(8):
            remote(
                win_ref.at[:, wide_slice(g * 4 * frows + pp * frows, frows, frows)],
                s.win.at[wide_slice(wrow, rows, rows), pl.ds(g * frows, frows)],
                (N.wi1, k), (N.wi1, k), dev(c, z, pp),
            )
        sent(s.win.at[pl.ds(0, rows)], (N.wi1, k))
    for k in (1, 2, 3):
        arrived(s.smalls.at[0, 0, 0], (N.smz, k))
    for k in (1, 2, 3):
        for zz in range(PLANES):
            ref = s.smalls.at[c, zz, p]
            remote(ref, ref, N.smp, (N.smp, k), dev(c, z, plane_peers[k]))
    sent(s.smalls.at[0, pl.ds(0, 3)], N.smp)
    for k in (1, 2, 3):
        arrived(s.inf.at[0], (N.inf, k))
    inf_half = s.inf.at[wide_slice(c * 4, 4, 4)]
    remote(inf_half, inf_half, N.infs, N.infs, dev(other, z, p))
    sent(inf_half, N.infs)
    for k in (1, 2, 3):
        arrived(s.smalls.at[0, 0], (N.smp, k))
    remote(s.smalls.at[c], s.smalls.at[c], N.sms, N.sms, dev(other, z, p))
    sent(s.smalls.at[0], N.sms)
    arrived(wo_ref, N.wo0)
    for k in (1, 2, 3):
        arrived(wo_ref, (N.woz, k))
    arrived(s.win.at[pl.ds(0, rows)], N.wi0)
    for k in (1, 2, 3):
        arrived(s.win.at[pl.ds(0, rows)], (N.wi1, k))
    wi_block = s.win.at[wide_slice(zrow, zrows, zrows)]
    for k in (1, 2, 3):
        remote(wi_block, wi_block, N.wi2, (N.wi2, k), dev(c, z_peers[k], p))
    sent(s.win.at[pl.ds(0, 3 * zrows)], N.wi2)
    remote(wi_block, wi_block, N.wi3, N.wi3, dev(other, z, p))
    fblock = (c * 4 + z) * frows
    f_ref = s.wfo.at[wide_slice(fblock, frows, frows)]
    pltpu.make_async_copy(wfo_ref, f_ref, sem(RECV, N.wf0)).start()
    for k in (1, 2, 3):
        remote(wfo_ref, f_ref, N.wf2, (N.wf2, k), dev(c, z_peers[k], p))
    sent(s.wfo.at[pl.ds(0, 3 * frows)], N.wf2)
    remote(wfo_ref, f_ref, N.wf3, N.wf3, dev(other, z, p))

    arrived(s.smalls.at[0], N.sms)
    pieces = s.smalls[...].reshape(512, 128)
    lane = lax.broadcasted_iota(jnp.int32, (128, model), 1)
    sub = lax.broadcasted_iota(jnp.int32, (128, model), 0)
    spread = jnp.where(lane % rows == sub, 1.0, 0.0).astype(BF16)
    laid = mm(pieces, spread)
    lane2 = lax.broadcasted_iota(jnp.int32, (512, model), 1)
    sub2 = lax.broadcasted_iota(jnp.int32, (512, model), 0)
    laid = jnp.where(lane2 // rows == sub2 // 16, laid, 0.0)
    s.vec[...] = jnp.sum(laid.reshape(32, 16, model), axis=0)
    for g in range(8):
        s.ffb[:, pl.ds(g * frows, frows)] = s.smalls[g // 4, g % 4, p].astype(F32)
    arrived(inf_half, N.infs)
    code_hot = []
    for g in range(8):
        code_hot.append(jnp.where(s.inf[g][1:2, :] == items + 1.0, 1.0, 0.0))
    seg_hot = []
    for g in range(4):
        seg_hot.append(jnp.where(s.inf[c * 4 + g][0:1, :] == items + 1.0, 1.0, 0.0))
    code_hot = jnp.concatenate(code_hot, axis=1)
    seg_hot = jnp.concatenate(seg_hot, axis=1)
    s.bias[...] = (mm(seg_hot, code_hot, 0, 0) - 1.0) * -NEGATIVE

    for k in (1, 2, 3):
        arrived(s.wqkv.at[pl.ds(0, zrows)], (N.wq2, k))
        block = s.wqkv.at[wide_slice(c * half + z_back[k] * zrows, zrows, zrows)]
        remote(block, block, N.wq3, N.wq3, dev(other, z, p))
    sent(s.wqkv.at[pl.ds(0, half)], N.wq3)
    for zz in range(PLANES):
        block = s.wo.at[wide_slice((c * 16 + zz * 4 + p) * rows, rows, rows)]
        for k in (1, 2, 3):
            remote(block, block, N.wop, (N.wop, k), dev(c, z, plane_peers[k]))
    sent(s.wo.at[pl.ds(0, 3 * PLANES * rows)], N.wop)
    arrived(s.wqkv.at[pl.ds(0, half)], N.wq3)

    q_bias = s.vec[0:1, wide_slice(p * wid, wid, wid)]
    v_bias = s.vec[1:2, wide_slice(p * wid, wid, wid)]
    for k in range(4):
        pp = plane_peers[k]
        here = wide_slice(pp * chunk, chunk, chunk)
        if k:
            arrived(s.slow.at[pl.ds(0, chunk)], (N.slow, k))
        low_chunk = s.slow[here, :]
        krow = wide_slice(c * toks + pp * chunk, chunk, chunk)
        s.kv[krow, 0:wid] = mm(low_chunk, s.wqkv[:, wid:2 * wid]).astype(BF16)
        s.kv[krow, wid:2 * wid] = (mm(low_chunk, s.wqkv[:, 2 * wid:3 * wid]) + v_bias).astype(BF16)
        remote(s.kv.at[krow], s.kv.at[krow], N.kv, N.kv, dev(other, z, p))
        s.q[here, :] = (mm(low_chunk, s.wqkv[:, 0:wid]) + q_bias).astype(BF16)
    kv_half = s.kv.at[wide_slice(c * toks, toks, toks)]
    sent(kv_half, N.kv)

    for k in (1, 2, 3):
        arrived(s.wo.at[pl.ds(0, PLANES * rows)], (N.wop, k))
    wo_half = s.wo.at[wide_slice(c * half, half, half)]
    remote(wo_half, wo_half, N.wos, N.wos, dev(other, z, p))
    sent(wo_half, N.wos)
    arrived(kv_half, N.kv)

    scale = HEAD ** (-0.5)
    qt = TILE
    s.att[...] = jnp.zeros_like(s.att)

    def head_mask(h, n):
        return lax.broadcasted_iota(jnp.int32, (n, wid), 1) // HEAD == h

    def attend(step, carry):
        h = step % heads
        t = step // heads
        here = wide_slice(t * qt, qt, qt)
        mask = head_mask(h, qt)
        queries = jnp.where(mask, s.q[here, :].astype(F32) * scale, 0.0).astype(BF16)
        scores = mm(queries, s.kv[:, 0:wid], 1, 1) + s.bias[here, :]
        top = jnp.max(scores, axis=-1, keepdims=True)
        weights = jnp.exp(scores - top)
        total = jnp.sum(weights, axis=-1, keepdims=True)
        result = mm(weights.astype(BF16), s.kv[:, wid:2 * wid]) / total
        s.att[here, :] = jnp.where(mask, result, s.att[here, :])
        s.lse[h, here, :] = top + jnp.log(total)
        return carry

    lax.fori_loop(0, heads * (toks // qt), attend, 0)
    s.attl[...] = s.att[...].astype(BF16)
    for k in (1, 2, 3):
        pp = plane_peers[k]
        remote(
            s.attl.at[wide_slice(pp * chunk, chunk, chunk)],
            s.attx.at[:, wide_slice(p * wid, wid, wid)],
            N.attx, (N.attx, k), dev(c, z, pp),
        )
    sent(s.attl.at[pl.ds(0, 3 * chunk)], N.attx)
    s.attx[:, wide_slice(p * wid, wid, wid)] = s.attl[own_rows, :]

    for k in (1, 2, 3):
        arrived(s.win.at[pl.ds(0, zrows)], (N.wi2, k))
        block = s.win.at[wide_slice(c * half + z_back[k] * zrows, zrows, zrows)]
        remote(block, block, N.wi3, N.wi3, dev(other, z, p))
    sent(s.win.at[pl.ds(0, half)], N.wi3)

    arrived(s.wo.at[pl.ds(0, half)], N.wos)
    for k in (1, 2, 3):
        arrived(s.attl.at[pl.ds(0, chunk)], (N.attx, k))

    def row_vec(r):
        return s.vec[r:r + 1, :]

    def normalize_rows(hidden_rows):
        centered = hidden_rows - jnp.mean(hidden_rows, axis=-1, keepdims=True)
        inverse = lax.rsqrt(jnp.mean(centered * centered, axis=-1, keepdims=True) + EPSILON)
        return centered * inverse, inverse

    branch = mm(s.attx[...], s.wo[...]) + row_vec(2)
    normed, inverse = normalize_rows(s.sres[...] + branch)
    s.n1[...] = normed
    s.inv1[...] = inverse
    after = normed * row_vec(3) + row_vec(4)
    s.aft[...] = after
    s.hid[own_rows, :] = after.astype(BF16)
    plane_gather(s.hid, N.hid)

    arrived(wfo_ref, N.wf0)
    for k in (1, 2, 3):
        arrived(s.wfo.at[pl.ds(0, frows)], (N.wf2, k))
        block = s.wfo.at[wide_slice((c * 4 + z_back[k]) * frows, frows, frows)]
        remote(block, block, N.wf3, N.wf3, dev(other, z, p))
    sent(s.wfo.at[pl.ds(0, 4 * frows)], N.wf3)
    arrived(s.win.at[pl.ds(0, half)], N.wi3)

    def ffn_first(here):
        def one(n, carry):
            cols = wide_slice(n * TILE, TILE, TILE)
            acc = mm(s.hid[here, :], s.win[:, cols]) + s.ffb[8:9, cols]
            phi = 0.5 * (1.0 + lax.erf(acc * (2.0 ** -0.5)))
            s.act[here, cols] = (acc * phi).astype(BF16)
            s.pre[here, cols] = phi + acc * jnp.exp(-0.5 * acc * acc) * (1.0 / math.sqrt(2.0 * math.pi))
            return carry
        lax.fori_loop(0, units // TILE, one, 0)

    def column_tiles(fn, total, dst, dst_rows=None):
        def one(n, carry):
            cols = wide_slice(n * TILE, TILE, TILE)
            value = fn(cols).astype(dst.dtype)
            if dst_rows is None:
                dst[:, cols] = value
            else:
                dst[dst_rows, cols] = value
            return carry
        lax.fori_loop(0, total // TILE, one, 0)

    def plane_scatter_step(k, fn, name):
        if k:
            column_tiles(fn, model, s.fs.at[k])
            remote(s.fs.at[k], s.fr.at[k], name, (name, k), dev(c, z, plane_peers[k]))
        else:
            column_tiles(fn, model, s.own)

    def plane_scatter_sum(name):
        total = s.own[...]
        for k in (1, 2, 3):
            arrived(s.fr.at[k], (name, k))
            total = total + s.fr[k].astype(F32)
        return total

    def plane_sent_now(name):
        pltpu.make_async_copy(s.fs.at[pl.ds(0, 3)], s.fs.at[pl.ds(0, 3)], sem(SEND, name)).wait()

    def chunk_rows(k):
        return wide_slice(plane_peers[k] * chunk, chunk, chunk)

    for k in range(4):
        here = chunk_rows(k)
        if k:
            arrived(s.hid.at[pl.ds(0, chunk)], (N.hid, k))
        ffn_first(here)
        if k == 0:
            arrived(s.wfo.at[pl.ds(0, 4 * frows)], N.wf3)
        plane_scatter_step(k, lambda cols: mm(s.act[here, :], s.wfo[:, cols]), N.rs1)

    branch = plane_scatter_sum(N.rs1) + row_vec(5)
    normed2, inverse2 = normalize_rows(s.aft[...] + branch)
    gain2 = row_vec(6)
    s.outl[...] = (normed2 * gain2 + row_vec(7)).astype(BF16)
    arrived(s.cin, N.c)
    upstream = s.cin[...].astype(F32)
    s.smg[...] = jnp.zeros_like(s.smg)
    s.smg[6:7, :] = jnp.sum(upstream * normed2, axis=0, keepdims=True)
    s.smg[7:8, :] = jnp.sum(upstream, axis=0, keepdims=True)

    def norm_back(up, normed_rows, inverse_rows, gain):
        scaled = up * gain
        return inverse_rows * (
            scaled
            - jnp.mean(scaled, axis=-1, keepdims=True)
            - normed_rows * jnp.mean(scaled * normed_rows, axis=-1, keepdims=True)
        )

    second = norm_back(upstream, normed2, inverse2, gain2)
    s.second[...] = second
    second_low = second.astype(BF16)
    s.bg[own_rows, :] = second_low
    plane_gather(s.bg, N.bg)
    s.smg[5:6, :] = jnp.sum(second_low.astype(F32), axis=0, keepdims=True)

    def send_home(src, dst, name):
        for i in range(2):
            is_self = jnp.logical_and(home == c, 2 * c + i == z)
            maybe_local(
                src.at[pl.ds(i * tok, tok)], dst.at[slot], (name, i), name,
                dev(home, 2 * c + i, p), is_self,
            )

    send_home(s.outl, s.outr, N.out)

    def ffn_back(here):
        def one(n, carry):
            cols = wide_slice(n * TILE, TILE, TILE)
            acc = mm(s.bg[here, :], s.wfo[cols, :], 1, 1)
            s.pg[here, cols] = (acc * s.pre[here, cols]).astype(BF16)
            return carry
        lax.fori_loop(0, units // TILE, one, 0)

    plane_sent_now(N.rs1)
    for k in range(4):
        here = chunk_rows(k)
        if k:
            arrived(s.bg.at[pl.ds(0, chunk)], (N.bg, k))
        ffn_back(here)
        plane_scatter_step(k, lambda cols: mm(s.pg[here, :], s.win[cols, :], 1, 1), N.rs2)

    def grad_sibling(lhs, rhs, buf_s, name):
        def one(m, carry):
            at = wide_slice(m * TILE, TILE, TILE)
            cols = wide_slice(other * half + m * TILE, TILE, TILE)
            buf_s[at, :] = mm(lhs[:, cols], rhs[...], 0, 0).astype(BF16)
            return carry
        lax.fori_loop(0, half // TILE, one, 0)

    def sibling_send(buf_s, buf_r, name):
        remote(buf_s, buf_r, name, name, dev(other, z, p))
        sent(buf_s, name)

    def grad_own(lhs, rhs, buf_r, buf_o, buf_zs, buf_zr, name):
        arrived(buf_r, name)
        for k in (1, 2, 3, 0):
            at = wide_slice(z_peers[k] * zrows, zrows, zrows)
            cols = wide_slice(c * half + z_peers[k] * zrows, zrows, zrows)
            value = mm(lhs[:, cols], rhs[...], 0, 0) + buf_r[at, :].astype(F32)
            if k:
                buf_zs[k] = value.astype(BF16)
                remote(buf_zs.at[k], buf_zr.at[k], (name, N.z), (name, N.z, k), dev(c, z_peers[k], p))
            else:
                buf_o[...] = value
        sent(buf_zs.at[pl.ds(0, 3)], (name, N.z))

    grad_sibling(s.act, s.bg, s.gfo_s, N.gfo)
    sibling_send(s.gfo_s, s.gfo_r, N.gfo)
    grad_sibling(s.hid, s.pg, s.gwi_s, N.gwi)
    sibling_send(s.gwi_s, s.gwi_r, N.gwi)
    s.smg[8:9, :] = jnp.sum(s.pg[...].astype(F32), axis=0, keepdims=True)

    hidden_grad = s.second[...] + plane_scatter_sum(N.rs2)
    normed = s.n1[...]
    s.smg[3:4, :] = jnp.sum(hidden_grad * normed, axis=0, keepdims=True)
    s.smg[4:5, :] = jnp.sum(hidden_grad, axis=0, keepdims=True)
    first = norm_back(hidden_grad, normed, s.inv1[...], row_vec(3))
    s.first[...] = first
    first_low = first.astype(BF16)
    s.agl[...] = first_low
    s.smg[2:3, :] = jnp.sum(first_low.astype(F32), axis=0, keepdims=True)
    column_tiles(lambda cols: mm(s.agl[...], s.wo[cols, :], 1, 1), model, s.ado)
    for k in (1, 2, 3):
        pp = plane_peers[k]
        remote(
            s.ado.at[:, wide_slice(pp * wid, wid, wid)],
            s.do.at[own_rows],
            N.do, (N.do, k), dev(c, z, pp),
        )
    sent(s.do.at[pl.ds(0, 3 * chunk)], N.do)
    s.do[own_rows, :] = s.ado[:, wide_slice(p * wid, wid, wid)]

    grad_own(s.act, s.bg, s.gfo_r, s.gfo_o, s.gfo_zs, s.gfo_zr, N.gfo)
    grad_own(s.hid, s.pg, s.gwi_r, s.gwi_o, s.gwi_zs, s.gwi_zr, N.gwi)
    grad_sibling(s.attx, s.agl, s.gwo_s, N.gwo)
    sibling_send(s.gwo_s, s.gwo_r, N.gwo)

    for k in (1, 2, 3):
        arrived(s.do.at[pl.ds(0, chunk)], (N.do, k))

    s.dq[...] = jnp.zeros_like(s.dq)
    s.dk[...] = jnp.zeros_like(s.dk)
    s.dv[...] = jnp.zeros_like(s.dv)

    def attend_back(step, carry):
        h = step % heads
        t = step // heads
        here = wide_slice(t * qt, qt, qt)
        mask = head_mask(h, qt)
        queries = jnp.where(mask, s.q[here, :].astype(F32) * scale, 0.0).astype(BF16)
        scores = mm(queries, s.kv[:, 0:wid], 1, 1) + s.bias[here, :]
        probs = jnp.exp(scores - s.lse[h, here, :])
        grads = jnp.where(mask, s.do[here, :].astype(F32), 0.0)
        residue = jnp.sum(grads * s.att[here, :], axis=-1, keepdims=True)
        grads = grads.astype(BF16)
        prob_grad = mm(grads, s.kv[:, wid:2 * wid], 1, 1)
        score_grad = (probs * (prob_grad - residue)).astype(BF16)
        s.dv[...] += mm(probs.astype(BF16), grads, 0, 0)
        s.dk[...] += mm(score_grad, queries, 0, 0)
        s.dq[here, :] += jnp.where(mask, mm(score_grad, s.kv[:, 0:wid]), 0.0)
        return carry

    lax.fori_loop(0, heads * (toks // qt), attend_back, 0)
    theirs = wide_slice(other * toks, toks, toks)
    mine = wide_slice(c * toks, toks, toks)
    s.dkvs[:, 0:wid] = s.dk[theirs, :].astype(BF16)
    s.dkvs[:, wid:2 * wid] = s.dv[theirs, :].astype(BF16)
    sibling_send(s.dkvs, s.dkvr, N.dkv)
    s.dqkv[:, 0:wid] = (s.dq[...] * scale).astype(BF16)

    arrived(s.gwo_r, N.gwo)

    def own_tile(m, carry):
        at = wide_slice(m * TILE, TILE, TILE)
        cols = wide_slice(c * half + m * TILE, TILE, TILE)
        value = mm(s.attx[:, cols], s.agl[...], 0, 0) + s.gwo_r[at, :].astype(F32)
        s.gwo_o[at, :] = value
        s.gwo_p[at, :] = value.astype(BF16)
        return carry

    lax.fori_loop(0, half // TILE, own_tile, 0)

    arrived(s.dkvr, N.dkv)
    s.dqkv[:, wid:2 * wid] = (s.dk[mine, :] + s.dkvr[:, 0:wid].astype(F32)).astype(BF16)
    s.dqkv[:, 2 * wid:3 * wid] = (s.dv[mine, :] + s.dkvr[:, wid:2 * wid].astype(F32)).astype(BF16)

    plane_sent_now(N.rs2)
    for k in (1, 2, 3, 0):
        here = chunk_rows(k)
        plane_scatter_step(k, lambda cols: mm(s.dqkv[here, :], s.wqkv[cols, :], 1, 1), N.rs3)

    grad_sibling(s.slow, s.dqkv, s.gqk_s, N.gqk)
    sibling_send(s.gqk_s, s.gqk_r, N.gqk)
    for k in (1, 2, 3):
        for zz in range(PLANES):
            remote(
                s.gwo_p.at[wide_slice(zz * zrows + plane_peers[k] * rows, rows, rows)],
                s.gwo_pr.at[k, zz],
                N.gwop, (N.gwop, k), dev(c, z, plane_peers[k]),
            )
    sent(s.gwo_p.at[pl.ds(0, 3 * PLANES * rows)], N.gwop)
    grad_own(s.slow, s.dqkv, s.gqk_r, s.gqk_o, s.gqk_zs, s.gqk_zr, N.gqk)

    low_sum = jnp.sum(s.dqkv[...].astype(F32), axis=0, keepdims=True)
    pcols = wide_slice(p * wid, wid, wid)
    s.smg[0:1, pcols] = low_sum[:, 0:wid]
    s.smg[1:2, pcols] = low_sum[:, 2 * wid:3 * wid]
    for cc in range(2):
        for k in range(4):
            if cc == 0 and k == 0:
                continue
            tc = other if cc else c
            lanes = wide_slice((tc * 4 + z_peers[k]) * 128, 128, 128)
            remote(s.smg.at[:, lanes], s.sma.at[cc * 4 + k], N.sma, (N.sma, cc, k), dev(tc, z_peers[k], p))
    sent(s.smg.at[:, pl.ds(0, 7 * 128)], N.sma)

    total = s.first[...] + plane_scatter_sum(N.rs3)
    s.igl[...] = total.astype(BF16)
    send_home(s.igl, s.igr, N.ig)

    for k in (1, 2, 3):
        arrived(s.gwo_pr.at[k], (N.gwop, k))

    def gwo_total(zz):
        value = s.gwo_o[wide_slice(zz * zrows + p * rows, rows, rows), :]
        for k in (1, 2, 3):
            value = value + s.gwo_pr[k, zz].astype(F32)
        return value

    for k in (1, 2, 3):
        s.gwo_zs[k] = gwo_total(z_peers[k]).astype(BF16)
        remote(s.gwo_zs.at[k], s.gwo_zr.at[k], N.gwoz, (N.gwoz, k), dev(c, z_peers[k], p))
    sent(s.gwo_zs.at[pl.ds(0, 3)], N.gwoz)
    dwo_ref[...] = gwo_total(z)

    def z_total(buf_o, buf_zr, name):
        total = buf_o[...]
        for k in (1, 2, 3):
            arrived(buf_zr.at[k], (name, N.z, k))
            total = total + buf_zr[k].astype(F32)
        return total

    def plane_rows(buf_p, buf_pr, name):
        for k in (1, 2, 3):
            remote(
                buf_p.at[wide_slice(plane_peers[k] * rows, rows, rows)], buf_pr.at[k],
                name, (name, k), dev(c, z, plane_peers[k]),
            )
        sent(buf_p.at[pl.ds(0, 3 * rows)], name)

    s.gwi_o[...] = z_total(s.gwi_o, s.gwi_zr, N.gwi)
    s.gwi_p[...] = s.gwi_o[...].astype(BF16)
    plane_rows(s.gwi_p, s.gwi_pr, N.gwip)
    dwfo_ref[...] = z_total(s.gfo_o, s.gfo_zr, N.gfo)

    part = s.smg[:, wide_slice((c * 4 + z) * 128, 128, 128)]
    for cc in range(2):
        for k in range(4):
            if cc == 0 and k == 0:
                continue
            arrived(s.sma.at[cc * 4 + k], (N.sma, cc, k))
            part = part + s.sma[cc * 4 + k]
    s.smb[...] = part
    for k in (1, 2, 3):
        remote(s.smb, s.smb_r.at[k], N.smb, (N.smb, k), dev(c, z, plane_peers[k]))
    sent(s.smb_r.at[pl.ds(0, 3)], N.smb)

    s.gqk_o[...] = z_total(s.gqk_o, s.gqk_zr, N.gqk)
    s.gqk_p[...] = s.gqk_o[...].astype(BF16)
    plane_rows(s.gqk_p, s.gqk_pr, N.gqkp)

    arrived(s.outr, N.out)
    out_ref[...] = s.outr[...]

    for k in range(4):
        if k:
            arrived(s.gwi_pr.at[k], (N.gwip, k))
        pp = plane_peers[k]
        for g in range(8):
            piece_cols = slice(g * frows, (g + 1) * frows)
            if k:
                value = s.gwi_pr[k, :, piece_cols].astype(F32)
            else:
                value = s.gwi_o[wide_slice(p * rows, rows, rows), piece_cols]
            dwin_ref[:, wide_slice(g * 4 * frows + pp * frows, frows, frows)] = value
    for k in (1, 2, 3):
        arrived(s.gwo_zr.at[k], (N.gwoz, k))
        dwo_ref[...] += s.gwo_zr[k].astype(F32)
    all_rows = s.smb[...]
    for k in (1, 2, 3):
        arrived(s.smb_r.at[k], (N.smb, k))
        all_rows = all_rows + s.smb_r[k]
    row_ids = lax.broadcasted_iota(jnp.int32, (16, 128), 0)
    sg_ref[...] = jnp.where(row_ids == 8, s.smb[...], all_rows)
    for k in range(4):
        if k:
            arrived(s.gqk_pr.at[k], (N.gqkp, k))
        pp = plane_peers[k]
        for t in range(3):
            piece_cols = slice(t * wid, (t + 1) * wid)
            if k:
                value = s.gqk_pr[k, :, piece_cols].astype(F32)
            else:
                value = s.gqk_o[wide_slice(p * rows, rows, rows), piece_cols]
            dwqkv_ref[:, wide_slice(t * model + pp * wid, wid, wid)] = value
    arrived(s.igr, N.ig)
    ig_ref[...] = s.igr[...]

    @pl.when(table_here)
    def _():
        handle = sem(SEND, N.tbl)
        pltpu.make_async_copy(s.tbl, s.tbl, handle).wait()

    plane_sent_now(N.rs3)
    flush_sent()


def fused_local(
    inputs, segments, pad_mask, timesteps, w_qkv, bias_query, bias_value, w_attn_out, bias_attn_out,
    ln1_gain, ln1_shift, w_ffn_in, bias_ffn_in, w_ffn_out, bias_ffn_out, ln2_gain, ln2_shift, cotangent,
):
    _, tok, model = inputs.shape
    hidden = w_ffn_in.shape[1]
    rows = w_qkv.shape[0]
    blk = lax.axis_index("blk")
    half_width = model // 2
    frequency = jnp.exp(
        jnp.arange(half_width, dtype=F32) * (-math.log(10000.0) / half_width)
    )
    angles = timesteps.astype(F32)[..., None] * (100.0 / TSTEPS) * frequency
    table = jnp.concatenate([jnp.sin(angles), jnp.cos(angles)], axis=-1)
    vectors = jnp.stack(
        [bias_query, bias_value, bias_attn_out, ln1_gain, ln1_shift, bias_ffn_out, ln2_gain, ln2_shift]
    )
    small = jnp.concatenate(
        [
            jnp.pad(vectors, ((0, 0), (0, 128 - rows))),
            bias_ffn_in[None],
            jnp.zeros((7, 128), BF16),
        ]
    )
    codes = jnp.where(pad_mask == 1, segments, -1)
    marks = jnp.stack([segments, codes], axis=1).astype(F32) + 1.0
    odd = (blk // PLANE) % 2 == 1
    marks = jnp.concatenate([jnp.where(odd, 0.0, marks), jnp.where(odd, marks, 0.0)], axis=-1)
    info = jnp.pad(marks, ((0, 0), (0, 6), (0, 0)))

    plan = scratch_plan(tok, model, hidden)
    vmem = pl.BlockSpec(memory_space=pltpu.VMEM)
    outs = pl.pallas_call(
        functools.partial(fused, plan, tok, model, hidden),
        out_shape=(
            jax.ShapeDtypeStruct((2, tok, model), BF16),
            jax.ShapeDtypeStruct((2, tok, model), BF16),
            jax.ShapeDtypeStruct((rows, 3 * model), F32),
            jax.ShapeDtypeStruct((rows, model), F32),
            jax.ShapeDtypeStruct((rows, hidden), F32),
            jax.ShapeDtypeStruct((hidden // 32, model), F32),
            jax.ShapeDtypeStruct((16, 128), F32),
        ),
        in_specs=[vmem] * 9,
        out_specs=[vmem] * 7,
        scratch_shapes=[pltpu.VMEM(shape, dtype) for shape, dtype in plan.values()]
        + [pltpu.SemaphoreType.DMA((N_SEND,)), pltpu.SemaphoreType.DMA((N_RECV,))],
        compiler_params=pltpu.CompilerParams(
            collective_id=0, has_side_effects=True, vmem_limit_bytes=63 * 1024 * 1024
        ),
    )(inputs, cotangent, table, small, info, w_qkv, w_attn_out, w_ffn_in, w_ffn_out)
    out, input_grad, g_qkv, g_out, g_in, g_down, g_small = outs
    mine = lax.dynamic_slice(g_small, (0, (blk % PLANE) * rows), (8, rows))
    return (
        out, input_grad, g_qkv, mine[0], mine[1], g_out, mine[2], mine[3], mine[4],
        g_in, g_small[8], g_down, mine[5], mine[6], mine[7],
    )


def layer(*args):
    inputs, w_qkv, w_ffn_out = args[0], args[4], args[13]
    fits = (
        lax.axis_size("dp") == 2
        and lax.axis_size("blk") == PLANE * PLANES
        and inputs.shape[0] == 2
        and inputs.shape[1] == 64
        and w_qkv.shape[0] * PLANE == 128
        and w_ffn_out.shape[0] == 128
        and args[3].shape[1] <= 8
    )
    return (fused_local if fits else local)(*args)


def solution(mesh):
    return jax.shard_map(
        layer,
        mesh=mesh,
        in_specs=(
            P("dp", "blk", None),
            P("dp", "blk"),
            P("dp", "blk"),
            P("dp", None),
            P(("dp", "blk"), None),
            P(("dp", "blk")),
            P(("dp", "blk")),
            P(("dp", "blk"), None),
            P(("dp", "blk")),
            P(("dp", "blk")),
            P(("dp", "blk")),
            P(("dp", "blk"), None),
            P(("dp", "blk")),
            P(("dp", "blk"), None),
            P(("dp", "blk")),
            P(("dp", "blk")),
            P(("dp", "blk")),
            P("dp", "blk", None),
        ),
        out_specs=(
            P("dp", "blk", None),
            P("dp", "blk", None),
            P(("dp", "blk"), None),
            P(("dp", "blk")),
            P(("dp", "blk")),
            P(("dp", "blk"), None),
            P(("dp", "blk")),
            P(("dp", "blk")),
            P(("dp", "blk")),
            P(("dp", "blk"), None),
            P(("dp", "blk")),
            P(("dp", "blk"), None),
            P(("dp", "blk")),
            P(("dp", "blk")),
            P(("dp", "blk")),
        ),
        check_vma=False,
    )
```

```python
import functools
import math

import jax
import jax.numpy as jnp
from jax import lax
from jax.experimental import pallas as pl
from jax.experimental.pallas import tpu as pltpu
from jax.sharding import PartitionSpec as P

HEADS = 16
HEAD = 64
TSTEPS = 5000


EPSILON = 1e-05
NEGATIVE = -1e30


def time_features(timesteps, segments, model_width):
    item_count = timesteps.shape[1]
    numbers = jnp.arange(item_count, dtype=jnp.int32)
    picked = jnp.sum(
        jnp.where(segments[:, :, None] == numbers[None, None, :], timesteps[:, None, :], 0), axis=-1
    )
    half_width = model_width // 2
    frequency = jnp.exp(
        jnp.arange(half_width, dtype=jnp.float32) * (-math.log(10000.0) / half_width)
    )
    angles = picked.astype(jnp.float32)[..., None] * (100.0 / TSTEPS) * frequency
    return jnp.concatenate([jnp.sin(angles), jnp.cos(angles)], axis=-1)


def normalize(hidden):
    centered = hidden - jnp.mean(hidden, axis=-1, keepdims=True)
    inverse = lax.rsqrt(jnp.mean(centered * centered, axis=-1, keepdims=True) + EPSILON)
    return (centered * inverse, inverse)


def norm_backward(upstream, normed, inverse, gain):
    scaled = upstream * gain
    return inverse * (
        scaled
        - jnp.mean(scaled, axis=-1, keepdims=True)
        - normed * jnp.mean(scaled * normed, axis=-1, keepdims=True)
    )


def exact_gelu(values):
    return jax.nn.gelu(values, approximate=False)


def local(
    inputs,
    segments,
    pad_mask,
    timesteps,
    w_qkv,
    bias_query,
    bias_value,
    w_attn_out,
    bias_attn_out,
    ln1_gain,
    ln1_shift,
    w_ffn_in,
    bias_ffn_in,
    w_ffn_out,
    bias_ffn_out,
    ln2_gain,
    ln2_shift,
    cotangent,
):
    row_count, tok_count, model_width = inputs.shape
    flat_count = row_count * tok_count
    head_count = HEADS
    head_dim = HEAD
    scale = HEAD ** (-0.5)
    bf16 = jnp.bfloat16
    single = jnp.float32
    attn_full = (
        lax.all_gather(w_qkv, ("dp", "blk"), axis=0, tiled=True),
        lax.all_gather(bias_query, ("dp", "blk"), axis=0, tiled=True),
        lax.all_gather(bias_value, ("dp", "blk"), axis=0, tiled=True),
        lax.all_gather(w_attn_out, ("dp", "blk"), axis=0, tiled=True),
        lax.all_gather(bias_attn_out, ("dp", "blk"), axis=0, tiled=True),
        lax.all_gather(ln1_gain, ("dp", "blk"), axis=0, tiled=True),
        lax.all_gather(ln1_shift, ("dp", "blk"), axis=0, tiled=True),
    )
    qkv_weight, query_bias, value_bias, out_weight, out_bias, gain_one, shift_one = attn_full
    embedded = time_features(timesteps, segments, model_width)
    start_flat = (inputs.astype(single) + embedded).reshape(flat_count, model_width)
    start_low = start_flat.astype(bf16)
    projected = jnp.dot(start_low, qkv_weight, preferred_element_type=single)
    query_send = (
        (projected[:, :model_width] + query_bias.astype(single))
        .astype(bf16)
        .reshape(row_count, tok_count, model_width)
    )
    key_send = (
        projected[:, model_width : 2 * model_width]
        .astype(bf16)
        .reshape(row_count, tok_count, model_width)
    )
    value_send = (
        (projected[:, 2 * model_width :] + value_bias.astype(single))
        .astype(bf16)
        .reshape(row_count, tok_count, model_width)
    )
    query_heads = query_send.reshape(row_count, tok_count, head_count, head_dim)
    key_heads = key_send.reshape(row_count, tok_count, head_count, head_dim)
    value_heads = value_send.reshape(row_count, tok_count, head_count, head_dim)
    codes = jnp.where(pad_mask == 1, segments, -1)
    code_float = codes.astype(single)
    seg_float = segments.astype(single)
    code_send = codes.astype(bf16)
    seg_send = segments.astype(bf16)

    def split_heads(piece):
        return piece.reshape(piece.shape[0], piece.shape[1], head_count, head_dim)

    piece = (
        lax.all_gather(key_send, "blk", axis=1, tiled=True),
        lax.all_gather(value_send, "blk", axis=1, tiled=True),
        lax.all_gather(code_send, "blk", axis=1, tiled=True),
    )
    run_max = jnp.full((row_count, tok_count, head_count), NEGATIVE, single)
    piece_keys = split_heads(piece[0])
    piece_values = split_heads(piece[1])
    scores = (
        jnp.einsum("rqhe,rkhe->rqhk", query_heads, piece_keys, preferred_element_type=single)
        * scale
    )
    valid = seg_float[:, :, None, None] == piece[2].astype(single)[:, None, None, :]
    masked = jnp.where(valid, scores, NEGATIVE)
    new_max = jnp.maximum(run_max, jnp.max(masked, axis=-1))
    weights = jnp.where(valid, jnp.exp(masked - new_max[..., None]), 0.0)
    run_sum = jnp.sum(weights, axis=-1)
    run_acc = jnp.einsum(
        "rqhk,rkhe->rqhe", weights.astype(bf16), piece_values, preferred_element_type=single
    )
    run_max, run_sum, run_acc = (new_max, run_sum, run_acc)
    log_total = run_max + jnp.log(run_sum)
    attended = run_acc / run_sum[..., None]
    attended_low = attended.reshape(flat_count, model_width).astype(bf16)
    attn_branch = jnp.dot(
        attended_low, out_weight, preferred_element_type=single
    ) + out_bias.astype(single)
    normed_one, inverse_one = normalize(start_flat + attn_branch)
    gain_one_f = gain_one.astype(single)
    after_attn = normed_one * gain_one_f + shift_one.astype(single)
    ffn_full = (
        lax.all_gather(w_ffn_in, ("dp", "blk"), axis=0, tiled=True),
        lax.all_gather(bias_ffn_in, ("dp", "blk"), axis=0, tiled=True),
        lax.all_gather(w_ffn_out, ("dp", "blk"), axis=0, tiled=True),
        lax.all_gather(bias_ffn_out, ("dp", "blk"), axis=0, tiled=True),
        lax.all_gather(ln2_gain, ("dp", "blk"), axis=0, tiled=True),
        lax.all_gather(ln2_shift, ("dp", "blk"), axis=0, tiled=True),
    )
    in_weight, in_bias, down_weight, down_bias, gain_two, shift_two = ffn_full
    hidden_low = after_attn.astype(bf16)
    pre_act = jnp.dot(hidden_low, in_weight, preferred_element_type=single) + in_bias.astype(single)
    activated, gelu_pull = jax.vjp(exact_gelu, pre_act)
    activated_low = activated.astype(bf16)
    branch = jnp.dot(activated_low, down_weight, preferred_element_type=single) + down_bias.astype(
        single
    )
    normed_two, inverse_two = normalize(after_attn + branch)
    gain_two_f = gain_two.astype(single)
    outputs = (
        (normed_two * gain_two_f + shift_two.astype(single))
        .astype(bf16)
        .reshape(row_count, tok_count, model_width)
    )
    ffn_back = (
        lax.all_gather(w_ffn_in, ("dp", "blk"), axis=0, tiled=True),
        lax.all_gather(w_ffn_out, ("dp", "blk"), axis=0, tiled=True),
    )
    in_weight_back, down_weight_back = ffn_back
    upstream = cotangent.astype(single).reshape(flat_count, model_width)
    gain_two_grad = jnp.sum(upstream * normed_two, axis=0)
    shift_two_grad = jnp.sum(upstream, axis=0)
    second_grad = norm_backward(upstream, normed_two, inverse_two, gain_two_f)
    branch_grad = second_grad.astype(bf16)
    down_weight_grad = jnp.einsum(
        "tf,td->fd", activated_low, branch_grad, preferred_element_type=single
    )
    down_bias_grad = jnp.sum(branch_grad.astype(single), axis=0)
    act_grad = jnp.einsum("td,fd->tf", branch_grad, down_weight_back, preferred_element_type=single)
    pre_grad = gelu_pull(act_grad)[0].astype(bf16)
    in_weight_grad = jnp.einsum("td,tf->df", hidden_low, pre_grad, preferred_element_type=single)
    in_bias_grad = jnp.sum(pre_grad.astype(single), axis=0)
    hidden_grad = second_grad + jnp.einsum(
        "tf,df->td", pre_grad, in_weight_back, preferred_element_type=single
    )
    gain_one_grad = jnp.sum(hidden_grad * normed_one, axis=0)
    shift_one_grad = jnp.sum(hidden_grad, axis=0)
    first_grad = norm_backward(hidden_grad, normed_one, inverse_one, gain_one_f)
    ffn_grads = (
        lax.psum_scatter(in_weight_grad, ("dp", "blk"), scatter_dimension=0, tiled=True),
        lax.psum_scatter(in_bias_grad, ("dp", "blk"), scatter_dimension=0, tiled=True),
        lax.psum_scatter(down_weight_grad, ("dp", "blk"), scatter_dimension=0, tiled=True),
        lax.psum_scatter(down_bias_grad, ("dp", "blk"), scatter_dimension=0, tiled=True),
        lax.psum_scatter(gain_two_grad, ("dp", "blk"), scatter_dimension=0, tiled=True),
        lax.psum_scatter(shift_two_grad, ("dp", "blk"), scatter_dimension=0, tiled=True),
    )
    attn_back = (
        lax.all_gather(w_qkv, ("dp", "blk"), axis=0, tiled=True),
        lax.all_gather(w_attn_out, ("dp", "blk"), axis=0, tiled=True),
    )
    qkv_weight_back, out_weight_back = attn_back
    attn_grad_low = first_grad.astype(bf16)
    out_weight_grad = jnp.einsum(
        "td,te->de", attended_low, attn_grad_low, preferred_element_type=single
    )
    out_bias_grad = jnp.sum(attn_grad_low.astype(single), axis=0)
    attended_grad = jnp.einsum(
        "te,de->td", attn_grad_low, out_weight_back, preferred_element_type=single
    ).astype(bf16)
    grad_send = attended_grad.reshape(row_count, tok_count, model_width)
    grad_heads = grad_send.reshape(row_count, tok_count, head_count, head_dim)
    residue = jnp.sum(grad_heads.astype(single) * attended, axis=-1)
    stats_full = (
        lax.all_gather(log_total, "blk", axis=1, tiled=True),
        lax.all_gather(residue, "blk", axis=1, tiled=True),
    )
    log_full, residue_full = stats_full
    piece = (
        lax.all_gather(key_send, "blk", axis=1, tiled=True),
        lax.all_gather(value_send, "blk", axis=1, tiled=True),
        lax.all_gather(code_send, "blk", axis=1, tiled=True),
    )
    piece_keys = split_heads(piece[0])
    piece_values = split_heads(piece[1])
    scores = (
        jnp.einsum("rqhe,rkhe->rqhk", query_heads, piece_keys, preferred_element_type=single)
        * scale
    )
    valid = seg_float[:, :, None, None] == piece[2].astype(single)[:, None, None, :]
    probs = jnp.exp(jnp.where(valid, scores - log_total[..., None], NEGATIVE))
    prob_grad = jnp.einsum(
        "rqhe,rkhe->rqhk", grad_heads, piece_values, preferred_element_type=single
    )
    score_grad = (probs * (prob_grad - residue[..., None])).astype(bf16)
    query_grad = (
        jnp.einsum("rqhk,rkhe->rqhe", score_grad, piece_keys, preferred_element_type=single) * scale
    )
    piece = (
        lax.all_gather(query_send, "blk", axis=1, tiled=True),
        lax.all_gather(grad_send, "blk", axis=1, tiled=True),
        lax.all_gather(seg_send, "blk", axis=1, tiled=True),
    )
    piece_queries = split_heads(piece[0])
    piece_grads = split_heads(piece[1])
    scores = (
        jnp.einsum("rqhe,rkhe->rqhk", piece_queries, key_heads, preferred_element_type=single)
        * scale
    )
    valid = piece[2].astype(single)[:, :, None, None] == code_float[:, None, None, :]
    probs = jnp.exp(jnp.where(valid, scores - log_full[..., None], NEGATIVE))
    value_acc = jnp.einsum(
        "rqhk,rqhe->rkhe", probs.astype(bf16), piece_grads, preferred_element_type=single
    )
    prob_grad = jnp.einsum(
        "rqhe,rkhe->rqhk", piece_grads, value_heads, preferred_element_type=single
    )
    score_grad = (probs * (prob_grad - residue_full[..., None])).astype(bf16)
    key_acc = (
        jnp.einsum("rqhk,rqhe->rkhe", score_grad, piece_queries, preferred_element_type=single)
        * scale
    )
    query_low = query_grad.astype(bf16).reshape(flat_count, model_width)
    key_low = key_acc.astype(bf16).reshape(flat_count, model_width)
    value_low = value_acc.astype(bf16).reshape(flat_count, model_width)
    qkv_grad = jnp.concatenate([query_low, key_low, value_low], axis=1)
    qkv_weight_grad = jnp.einsum("td,tc->dc", start_low, qkv_grad, preferred_element_type=single)
    query_bias_grad = jnp.sum(query_low.astype(single), axis=0)
    value_bias_grad = jnp.sum(value_low.astype(single), axis=0)
    input_grad = (
        first_grad
        + jnp.einsum("tc,dc->td", qkv_grad, qkv_weight_back, preferred_element_type=single)
    ).astype(bf16)
    input_grad = input_grad.reshape(row_count, tok_count, model_width)
    attn_grads = (
        lax.psum_scatter(qkv_weight_grad, ("dp", "blk"), scatter_dimension=0, tiled=True),
        lax.psum_scatter(query_bias_grad, ("dp", "blk"), scatter_dimension=0, tiled=True),
        lax.psum_scatter(value_bias_grad, ("dp", "blk"), scatter_dimension=0, tiled=True),
        lax.psum_scatter(out_weight_grad, ("dp", "blk"), scatter_dimension=0, tiled=True),
        lax.psum_scatter(out_bias_grad, ("dp", "blk"), scatter_dimension=0, tiled=True),
        lax.psum_scatter(gain_one_grad, ("dp", "blk"), scatter_dimension=0, tiled=True),
        lax.psum_scatter(shift_one_grad, ("dp", "blk"), scatter_dimension=0, tiled=True),
    )
    return (
        outputs,
        input_grad,
        attn_grads[0],
        attn_grads[1],
        attn_grads[2],
        attn_grads[3],
        attn_grads[4],
        attn_grads[5],
        attn_grads[6],
        ffn_grads[0],
        ffn_grads[1],
        ffn_grads[2],
        ffn_grads[3],
        ffn_grads[4],
        ffn_grads[5],
    )


MESH = pl.DeviceIdType.MESH
PLANE = 4
PLANES = 4
TILE = 256
BF16 = jnp.bfloat16
F32 = jnp.float32


def mm(left, right, left_dim=1, right_dim=0):
    return lax.dot_general(
        left, right, (((left_dim,), (right_dim,)), ((), ())), preferred_element_type=F32
    )


def wide_slice(start, size, step):
    return pl.ds(pl.multiple_of(start, step), size)


class Names:
    pass


class Labels:
    def __getattr__(self, name):
        return name


N = Labels()
SEND, RECV = 0, 1


def scratch_plan(tok, model, hidden):
    chunk = 2 * tok
    toks = PLANE * chunk
    keys = 2 * toks
    wid = model // PLANE
    units = hidden // PLANE
    rows = model // 32
    zrows = PLANE * rows
    half = PLANES * zrows
    return dict(
        xin=((chunk, model), BF16),
        cin=((chunk, model), BF16),
        tbl=((8, model), F32),
        inf_in=((2, 8, 128), F32),
        inf=((8, 8, 128), F32),
        smalls=((2, PLANES, PLANE, 16, 128), BF16),
        vec=((16, model), F32),
        ffb=((16, units), F32),
        wqkv=((model, 3 * wid), BF16),
        wo=((model, model), BF16),
        win=((model, units), BF16),
        wfo=((units, model), BF16),
        sres=((chunk, model), F32),
        slow=((toks, model), BF16),
        q=((toks, wid), BF16),
        kv=((keys, 2 * wid), BF16),
        bias=((toks, keys), F32),
        att=((toks, wid), F32),
        lse=((4, toks, 1), F32),
        attl=((toks, wid), BF16),
        attx=((chunk, model), BF16),
        n1=((chunk, model), F32),
        inv1=((chunk, 1), F32),
        aft=((chunk, model), F32),
        hid=((toks, model), BF16),
        pre=((toks, units), F32),
        act=((toks, units), BF16),
        fs=((PLANE, chunk, model), BF16),
        fr=((3, chunk, model), BF16),
        own=((chunk, model), F32),
        outl=((chunk, model), BF16),
        outr=((2, tok, model), BF16),
        second=((chunk, model), F32),
        bg=((toks, model), BF16),
        pg=((toks, units), BF16),
        first=((chunk, model), F32),
        agl=((chunk, model), BF16),
        ado=((chunk, model), BF16),
        do=((toks, wid), BF16),
        dq=((toks, wid), F32),
        dk=((keys, wid), F32),
        dv=((keys, wid), F32),
        dkvs=((toks, 2 * wid), BF16),
        dkvr=((toks, 2 * wid), BF16),
        dqkv=((toks, 3 * wid), BF16),
        igl=((chunk, model), BF16),
        igr=((2, tok, model), BF16),
        gfo_s=((half, model), BF16),
        gfo_r=((half, model), BF16),
        gfo_o=((zrows, model), F32),
        gfo_zs=((4, zrows, model), BF16),
        gfo_zr=((5, zrows, model), BF16),
        gwi_s=((half, units), BF16),
        gwi_r=((half, units), BF16),
        gwi_o=((zrows, units), F32),
        gwi_zs=((4, zrows, units), BF16),
        gwi_zr=((5, zrows, units), BF16),
        gwi_p=((zrows, units), BF16),
        gwi_pr=((4, rows, units), BF16),
        gqk_s=((half, 3 * wid), BF16),
        gqk_r=((half, 3 * wid), BF16),
        gqk_o=((zrows, 3 * wid), F32),
        gqk_zs=((4, zrows, 3 * wid), BF16),
        gqk_zr=((5, zrows, 3 * wid), BF16),
        gqk_p=((zrows, 3 * wid), BF16),
        gqk_pr=((4, rows, 3 * wid), BF16),
        gwo_s=((half, model), BF16),
        gwo_r=((half, model), BF16),
        gwo_o=((half, model), F32),
        gwo_p=((half, model), BF16),
        gwo_pr=((4, PLANES, rows, model), BF16),
        gwo_t=((rows, model), F32),
        gwo_zs=((4, rows, model), BF16),
        gwo_zr=((5, rows, model), BF16),
        smg=((16, model), F32),
        sma=((8, 16, 128), F32),
        smb=((16, 128), F32),
        smb_r=((4, 16, 128), F32),
    )


N_SEND = 160
N_RECV = 160


def fused(plan, tok, model, hidden, *refs):
    (x_ref, cot_ref, table_ref, small_ref, info_ref, wqkv_ref, wo_ref, win_ref, wfo_ref) = refs[:9]
    (out_ref, ig_ref, dwqkv_ref, dwo_ref, dwin_ref, dwfo_ref, sg_ref) = refs[9:16]
    s = Names()
    for name, ref in zip(plan, refs[16:]):
        setattr(s, name, ref)
    send_pool, recv_pool = refs[16 + len(plan):]

    chunk = 2 * tok
    toks = PLANE * chunk
    keys = 2 * toks
    wid = model // PLANE
    units = hidden // PLANE
    rows = model // 32
    zrows = PLANE * rows
    half = PLANES * zrows
    heads = wid // HEAD
    frows = hidden // 32

    c = lax.axis_index("dp")
    b = lax.axis_index("blk")
    z = b // PLANE
    p = b % PLANE
    y, x = p // 2, p % 2
    other = 1 - c
    plane_peers = [p, y * 2 + (1 - x), (1 - y) * 2 + x, PLANE - 1 - p]
    z_peers = [(z + k) % PLANES for k in range(PLANES)]
    z_back = [(z + PLANES - k) % PLANES for k in range(PLANES)]

    def dev(cc, zz, pp):
        return {"dp": cc, "blk": zz * PLANE + pp}

    used = ({}, {})

    def sem(kind, name):
        table = used[kind]
        if name not in table:
            table[name] = len(table)
            assert table[name] < (N_SEND, N_RECV)[kind]
        return (send_pool, recv_pool)[kind].at[table[name]]

    pending = []

    def remote(src, dst, send_name, recv_name, target):
        pltpu.make_async_remote_copy(
            src_ref=src,
            dst_ref=dst,
            send_sem=sem(SEND, send_name),
            recv_sem=sem(RECV, recv_name),
            device_id=target,
            device_id_type=MESH,
        ).start()

    def sent(ref, send_name, cond=None):
        pending.append((ref, send_name, cond))

    def flush_sent():
        for ref, send_name, cond in pending:
            def one():
                handle = sem(SEND, send_name)
                pltpu.make_async_copy(ref, ref, handle).wait()
            if cond is None:
                one()
            else:
                pl.when(cond)(one)
        pending.clear()

    def arrived(ref, recv_name):
        pltpu.make_async_copy(ref, ref, sem(RECV, recv_name)).wait()

    def maybe_local(src, dst, send_name, recv_name, target, is_self):
        send_handle = sem(SEND, send_name)
        recv_handle = sem(RECV, recv_name)

        @pl.when(is_self)
        def _():
            pltpu.make_async_copy(src, dst, recv_handle).start()

        @pl.when(jnp.logical_not(is_self))
        def _():
            pltpu.make_async_remote_copy(
                src_ref=src, dst_ref=dst, send_sem=send_handle, recv_sem=recv_handle,
                device_id=target, device_id_type=MESH,
            ).start()

        sent(src, send_name, jnp.logical_not(is_self))

    outer = z % 3 == 0
    inner = jnp.logical_not(outer)
    o_near, o_far, o_other = 1 + z // 3, 2 - z // 3, 3 - z
    i_near, i_far, i_pair = 3 * (z - 1), 6 - 3 * z, 3 - z

    class ZGather:
        def __init__(self, name, block, half_ref, src=None, sibling=True):
            self.name, self.block, self.src, self.sibling = name, block, src, sibling
            one = block(0)
            sent(one, (name, N.o), outer)
            for key in (N.i0, N.f0, N.i1, N.f1, N.f2):
                sent(one, (name, key), inner)
            if sibling:
                sent(half_ref, (name, N.s))
            self.half_ref = half_ref

        def send(self, zz, key, target, src=None):
            ref = self.block(zz)
            remote(ref if src is None else src, ref, (self.name, key), (self.name, key), dev(c, target, p))

        def over(self, zz, src=None):
            if self.sibling:
                ref = self.block(zz)
                remote(ref if src is None else src, ref, (self.name, N.s), (self.name, N.s), dev(other, z, p))

        def take(self, zz, key):
            arrived(self.block(zz), (self.name, key))

        def step0(self):
            @pl.when(outer)
            def _():
                self.send(z, N.o, o_near, self.src)

            @pl.when(inner)
            def _():
                self.send(z, N.i0, i_pair, self.src)
                self.send(z, N.f0, i_near, self.src)

            self.over(z, self.src)

        def step1(self):
            @pl.when(inner)
            def _():
                self.take(i_near, N.o)
                self.send(i_near, N.i1, i_pair)
                self.take(i_pair, N.i0)
                self.send(i_pair, N.f1, i_near)
                self.over(i_near)
                self.over(i_pair)

            @pl.when(outer)
            def _():
                self.take(o_near, N.f0)
                self.over(o_near)

        def step2(self):
            @pl.when(inner)
            def _():
                self.take(i_far, N.i1)
                self.send(i_far, N.f2, i_near)
                self.over(i_far)

            @pl.when(outer)
            def _():
                self.take(o_far, N.f1)
                self.over(o_far)

        def step3(self):
            @pl.when(outer)
            def _():
                self.take(o_other, N.f2)
                self.over(o_other)

        def done(self):
            arrived(self.half_ref, (self.name, N.s))

    class ZScatter:
        def __init__(self, name, part, keep, got):
            self.name, self.part, self.keep, self.got = name, part, keep, got
            for key in (N.o0, N.o1, N.o2):
                sent(part.at[0], (name, key), outer)
            for key in (N.i0, N.i1, N.f):
                sent(part.at[0], (name, key), inner)

        def put(self, zz, value):
            mine_block = zz == z

            @pl.when(mine_block)
            def _():
                self.keep[...] = value

            @pl.when(jnp.logical_not(mine_block))
            def _():
                self.part[zz] = value.astype(BF16)

        def send(self, zz, slot_id, key, target):
            remote(self.part.at[zz], self.got.at[slot_id], (self.name, key), (self.name, key), dev(c, target, p))

        def take(self, slot_id, key):
            arrived(self.got.at[slot_id], (self.name, key))
            return self.got[slot_id].astype(F32)

        def grow(self, zz, more):
            self.part[zz] = (self.part[zz].astype(F32) + more).astype(BF16)

        def step0(self):
            @pl.when(outer)
            def _():
                self.send(o_other, 0, N.o0, o_near)
                self.send(o_far, 1, N.o1, o_near)
                self.send(o_near, 2, N.o2, o_near)

        def step1(self):
            @pl.when(inner)
            def _():
                self.grow(i_far, self.take(0, N.o0))
                self.send(i_far, 3, N.i0, i_pair)
                self.grow(i_pair, self.take(1, N.o1))
                self.send(i_pair, 4, N.i1, i_pair)

        def step2(self):
            @pl.when(inner)
            def _():
                self.grow(i_near, self.take(3, N.i0))
                self.send(i_near, 0, N.f, i_near)
                self.keep[...] += self.take(2, N.o2)

        def step3(self):
            @pl.when(inner)
            def _():
                self.keep[...] += self.take(4, N.i1)

            @pl.when(outer)
            def _():
                self.keep[...] += self.take(0, N.f)

    class PlaneGather:
        def __init__(self, name, pieces, sizes):
            self.name, self.pieces, self.sizes = name, pieces, sizes
            for k in (1, 2):
                for h in (0, 1):
                    sent(sizes[h], (name, k, h))
                sent(sizes[2 - k], (name, 3, k))

        def send(self, pp, h, target, key, recv_key):
            for ref in self.pieces(pp, h):
                remote(ref, ref, (self.name,) + key, (self.name,) + recv_key, dev(c, z, target))

        def step0(self):
            for h in (1, 0):
                self.send(p, h, plane_peers[2], (2, h), (2, h))
                self.send(p, 1 - h, plane_peers[1], (1, 1 - h), (1, 1 - h))

        def step1(self):
            arrived(self.sizes[0], (self.name, 1, 0))
            self.send(plane_peers[1], 0, plane_peers[2], (3, 2), (3, 0))
            arrived(self.sizes[1], (self.name, 2, 1))
            self.send(plane_peers[2], 1, plane_peers[1], (3, 1), (3, 1))

        def done(self, k):
            if k in (1, 2):
                arrived(self.sizes[2 - k], (self.name, k, 2 - k))
            if k == 3:
                for h in (0, 1):
                    arrived(self.sizes[h], (self.name, 3, h))

    barrier = pltpu.get_barrier_semaphore()
    greeted = [dev(c, z, plane_peers[k]) for k in (1, 2, 3)]
    greeted += [dev(c, z_peers[k], p) for k in (1, 2, 3)]
    greeted += [dev(other, z_peers[k], p) for k in (0, 1, 2, 3)]
    for target in greeted:
        pl.semaphore_signal(barrier, inc=1, device_id=target, device_id_type=MESH)
    pl.semaphore_wait(barrier, len(greeted))

    home = z // 2
    slot = z % 2
    for i in range(2):
        plane_of = 2 * c + i
        is_self = jnp.logical_and(home == c, plane_of == z)
        target = dev(home, plane_of, p)
        maybe_local(x_ref.at[i], s.xin.at[wide_slice(slot * tok, tok, tok)], (N.x, i), N.x, target, is_self)
        maybe_local(info_ref.at[i], s.inf_in.at[slot], (N.i, i), N.i, target, is_self)

    table_here = home == c

    @pl.when(table_here)
    def _():
        remote(table_ref.at[slot], s.tbl, N.tbl, N.tbl, dev(other, z, p))
        s.tbl[...] = table_ref[slot]

    s.smalls[c, z, p] = small_ref[...]
    for k in (1, 2, 3):
        remote(small_ref, s.smalls.at[c, z, p], N.smz, (N.smz, k), dev(c, z_peers[k], p))
    sent(s.smalls.at[0, 0, pl.ds(0, 3)], N.smz)

    wrow = (c * 16 + z * 4 + p) * rows
    for t in range(3):
        pltpu.make_async_copy(
            wqkv_ref.at[:, wide_slice(t * model + p * wid, wid, wid)],
            s.wqkv.at[wide_slice(wrow, rows, rows), pl.ds(t * wid, wid)],
            sem(RECV, N.wq0),
        ).start()
    for k in (3, 1, 2):
        pp = plane_peers[k]
        for t in range(3):
            remote(
                wqkv_ref.at[:, wide_slice(t * model + pp * wid, wid, wid)],
                s.wqkv.at[wide_slice(wrow, rows, rows), pl.ds(t * wid, wid)],
                (N.wq1, k), (N.wq1, k), dev(c, z, pp),
            )
        sent(s.wqkv.at[pl.ds(0, rows)], (N.wq1, k))

    wo_block = s.wo.at[wide_slice(wrow, rows, rows)]
    pltpu.make_async_copy(wo_ref, wo_block, sem(RECV, N.wo0)).start()
    woz = ZGather(
        N.woz, lambda zz: s.wo.at[wide_slice((c * 16 + zz * 4 + p) * rows, rows, rows)], None, src=wo_ref, sibling=False
    )
    woz.step0()
    arrived(s.wqkv.at[pl.ds(0, rows)], N.wq0)
    for k in (1, 2, 3):
        arrived(s.wqkv.at[pl.ds(0, rows)], (N.wq1, k))
    zrow = c * half + z * zrows
    wq = ZGather(
        N.wq, lambda zz: s.wqkv.at[wide_slice(c * half + zz * zrows, zrows, zrows)], s.wqkv.at[pl.ds(0, half)]
    )
    wq.step0()

    for g in range(8):
        pltpu.make_async_copy(
            win_ref.at[:, wide_slice(g * 4 * frows + p * frows, frows, frows)],
            s.win.at[wide_slice(wrow, rows, rows), pl.ds(g * frows, frows)],
            sem(RECV, N.wi0),
        ).start()
    for k in (3, 1, 2):
        pp = plane_peers[k]
        for g in range(8):
            remote(
                win_ref.at[:, wide_slice(g * 4 * frows + pp * frows, frows, frows)],
                s.win.at[wide_slice(wrow, rows, rows), pl.ds(g * frows, frows)],
                (N.wi1, k), (N.wi1, k), dev(c, z, pp),
            )
        sent(s.win.at[pl.ds(0, rows)], (N.wi1, k))
    arrived(s.inf_in, N.i)
    info_own = s.inf_in[0] + s.inf_in[1]
    s.inf[c * 4 + p] = info_own
    for k in (1, 2, 3):
        blk_ref = s.inf.at[c * 4 + p]
        remote(blk_ref, blk_ref, N.inf, (N.inf, k), dev(c, z, plane_peers[k]))
    sent(s.inf.at[pl.ds(0, 3)], N.inf)

    @pl.when(jnp.logical_not(table_here))
    def _():
        arrived(s.tbl, N.tbl)

    arrived(s.xin, N.x)
    items = lax.broadcasted_iota(jnp.int32, (8, chunk), 0).astype(F32)
    onehot = jnp.where(info_own[0:1, :] == items + 1.0, 1.0, 0.0)
    embedded = lax.dot_general(
        onehot, s.tbl[...], (((0,), (0,)), ((), ())), precision=lax.Precision.HIGHEST,
        preferred_element_type=F32,
    )
    start_res = s.xin[...].astype(F32) + embedded
    s.sres[...] = start_res
    prow = p * chunk
    own_rows = wide_slice(prow, chunk, chunk)
    s.slow[own_rows, :] = start_res.astype(BF16)

    def plane_gather(ref, name):
        gather = PlaneGather(
            name,
            lambda pp, h: [ref.at[wide_slice(pp * chunk + h * tok, tok, tok)]],
            (ref.at[pl.ds(0, tok)], ref.at[pl.ds(0, tok)]),
        )
        gather.step0()
        return gather

    slow_gather = plane_gather(s.slow, N.slow)

    for k in (1, 2, 3):
        arrived(s.smalls.at[0, 0, 0], (N.smz, k))
    for k in (1, 2, 3):
        for zz in range(PLANES):
            ref = s.smalls.at[c, zz, p]
            remote(ref, ref, N.smp, (N.smp, k), dev(c, z, plane_peers[k]))
    sent(s.smalls.at[0, pl.ds(0, 3)], N.smp)
    wq.step1()
    woz.step1()
    for k in (1, 2, 3):
        arrived(s.inf.at[0], (N.inf, k))
    inf_half = s.inf.at[wide_slice(c * 4, 4, 4)]
    remote(inf_half, inf_half, N.infs, N.infs, dev(other, z, p))
    sent(inf_half, N.infs)
    slow_gather.step1()
    arrived(s.win.at[pl.ds(0, rows)], N.wi0)
    for k in (1, 2, 3):
        arrived(s.win.at[pl.ds(0, rows)], (N.wi1, k))
    wi = ZGather(
        N.wi, lambda zz: s.win.at[wide_slice(c * half + zz * zrows, zrows, zrows)], s.win.at[pl.ds(0, half)]
    )
    fblock = (c * 4 + z) * frows
    pltpu.make_async_copy(wfo_ref, s.wfo.at[wide_slice(fblock, frows, frows)], sem(RECV, N.wf0)).start()
    wf = ZGather(
        N.wf, lambda zz: s.wfo.at[wide_slice((c * 4 + zz) * frows, frows, frows)], s.wfo.at[pl.ds(0, 4 * frows)], src=wfo_ref
    )
    wq.step2()
    woz.step2()
    wi.step0()
    for k in (1, 2, 3):
        arrived(s.smalls.at[0, 0], (N.smp, k))
    remote(s.smalls.at[c], s.smalls.at[c], N.sms, N.sms, dev(other, z, p))
    sent(s.smalls.at[0], N.sms)
    arrived(s.smalls.at[0], N.sms)
    pieces = s.smalls[...].reshape(512, 128)
    lane = lax.broadcasted_iota(jnp.int32, (128, model), 1)
    sub = lax.broadcasted_iota(jnp.int32, (128, model), 0)
    spread = jnp.where(lane % rows == sub, 1.0, 0.0).astype(BF16)
    laid = mm(pieces, spread)
    lane2 = lax.broadcasted_iota(jnp.int32, (512, model), 1)
    sub2 = lax.broadcasted_iota(jnp.int32, (512, model), 0)
    laid = jnp.where(lane2 // rows == sub2 // 16, laid, 0.0)
    s.vec[...] = jnp.sum(laid.reshape(32, 16, model), axis=0)
    for g in range(8):
        s.ffb[:, pl.ds(g * frows, frows)] = s.smalls[g // 4, g % 4, p].astype(F32)
    arrived(inf_half, N.infs)
    code_hot = []
    for g in range(8):
        code_hot.append(jnp.where(s.inf[g][1:2, :] == items + 1.0, 1.0, 0.0))
    seg_hot = []
    for g in range(4):
        seg_hot.append(jnp.where(s.inf[c * 4 + g][0:1, :] == items + 1.0, 1.0, 0.0))
    code_hot = jnp.concatenate(code_hot, axis=1)
    seg_hot = jnp.concatenate(seg_hot, axis=1)
    s.bias[...] = (mm(seg_hot, code_hot, 0, 0) - 1.0) * -NEGATIVE

    wq.step3()
    wq.done()

    q_bias = s.vec[0:1, wide_slice(p * wid, wid, wid)]
    v_bias = s.vec[1:2, wide_slice(p * wid, wid, wid)]
    for k in range(4):
        pp = plane_peers[k]
        here = wide_slice(pp * chunk, chunk, chunk)
        slow_gather.done(k)
        low_chunk = s.slow[here, :]
        krow = wide_slice(c * toks + pp * chunk, chunk, chunk)
        s.kv[krow, 0:wid] = mm(low_chunk, s.wqkv[:, wid:2 * wid]).astype(BF16)
        s.kv[krow, wid:2 * wid] = (mm(low_chunk, s.wqkv[:, 2 * wid:3 * wid]) + v_bias).astype(BF16)
        remote(s.kv.at[krow], s.kv.at[krow], N.kv, N.kv, dev(other, z, p))
        s.q[here, :] = (mm(low_chunk, s.wqkv[:, 0:wid]) + q_bias).astype(BF16)
    kv_half = s.kv.at[wide_slice(c * toks, toks, toks)]
    sent(kv_half, N.kv)

    woz.step3()
    arrived(wo_ref, N.wo0)
    wop = PlaneGather(
        N.wop,
        lambda pp, h: [
            s.wo.at[wide_slice((c * 16 + (2 * h + g) * 4 + pp) * rows, rows, rows)] for g in range(2)
        ],
        (s.wo.at[pl.ds(0, 2 * rows)], s.wo.at[pl.ds(0, 2 * rows)]),
    )
    wop.step0()
    wi.step1()
    wf.step0()
    arrived(kv_half, N.kv)

    scale = HEAD ** (-0.5)
    qt = TILE
    s.att[...] = jnp.zeros_like(s.att)

    def head_mask(h, n):
        return lax.broadcasted_iota(jnp.int32, (n, wid), 1) // HEAD == h

    def attend(step, carry):
        h = step % heads
        t = step // heads
        here = wide_slice(t * qt, qt, qt)
        mask = head_mask(h, qt)
        queries = jnp.where(mask, s.q[here, :].astype(F32) * scale, 0.0).astype(BF16)
        scores = mm(queries, s.kv[:, 0:wid], 1, 1) + s.bias[here, :]
        top = jnp.max(scores, axis=-1, keepdims=True)
        weights = jnp.exp(scores - top)
        total = jnp.sum(weights, axis=-1, keepdims=True)
        result = mm(weights.astype(BF16), s.kv[:, wid:2 * wid]) / total
        s.att[here, :] = jnp.where(mask, result, s.att[here, :])
        s.lse[h, here, :] = top + jnp.log(total)
        return carry

    steps = heads * (toks // qt)
    lax.fori_loop(0, steps // 2, attend, 0)
    wop.step1()
    wf.step1()
    lax.fori_loop(steps // 2, steps, attend, 0)
    s.attl[...] = s.att[...].astype(BF16)
    for k in (1, 2, 3):
        pp = plane_peers[k]
        remote(
            s.attl.at[wide_slice(pp * chunk, chunk, chunk)],
            s.attx.at[:, wide_slice(p * wid, wid, wid)],
            N.attx, (N.attx, k), dev(c, z, pp),
        )
    sent(s.attl.at[pl.ds(0, 3 * chunk)], N.attx)
    s.attx[:, wide_slice(p * wid, wid, wid)] = s.attl[own_rows, :]

    wi.step2()
    for k in (1, 2, 3):
        wop.done(k)
    wo_half = s.wo.at[wide_slice(c * half, half, half)]
    remote(wo_half, wo_half, N.wos, N.wos, dev(other, z, p))
    sent(wo_half, N.wos)
    arrived(s.wo.at[pl.ds(0, half)], N.wos)
    for k in (1, 2, 3):
        arrived(s.attl.at[pl.ds(0, chunk)], (N.attx, k))

    def row_vec(r):
        return s.vec[r:r + 1, :]

    def normalize_rows(hidden_rows):
        centered = hidden_rows - jnp.mean(hidden_rows, axis=-1, keepdims=True)
        inverse = lax.rsqrt(jnp.mean(centered * centered, axis=-1, keepdims=True) + EPSILON)
        return centered * inverse, inverse

    branch = mm(s.attx[...], s.wo[...]) + row_vec(2)
    normed, inverse = normalize_rows(s.sres[...] + branch)
    s.n1[...] = normed
    s.inv1[...] = inverse
    after = normed * row_vec(3) + row_vec(4)
    s.aft[...] = after
    s.hid[own_rows, :] = after.astype(BF16)
    hid_gather = plane_gather(s.hid, N.hid)

    for i in range(2):
        plane_of = 2 * c + i
        is_self = jnp.logical_and(home == c, plane_of == z)
        target = dev(home, plane_of, p)
        maybe_local(cot_ref.at[i], s.cin.at[wide_slice(slot * tok, tok, tok)], (N.c, i), N.c, target, is_self)
    arrived(wfo_ref, N.wf0)
    wi.step3()
    wi.done()

    def ffn_first(here):
        def one(n, carry):
            cols = wide_slice(n * TILE, TILE, TILE)
            acc = mm(s.hid[here, :], s.win[:, cols]) + s.ffb[8:9, cols]
            phi = 0.5 * (1.0 + lax.erf(acc * (2.0 ** -0.5)))
            s.act[here, cols] = (acc * phi).astype(BF16)
            s.pre[here, cols] = phi + acc * jnp.exp(-0.5 * acc * acc) * (1.0 / math.sqrt(2.0 * math.pi))
            return carry
        lax.fori_loop(0, units // TILE, one, 0)

    def column_tiles(fn, total, dst, dst_rows=None):
        def one(n, carry):
            cols = wide_slice(n * TILE, TILE, TILE)
            value = fn(cols).astype(dst.dtype)
            if dst_rows is None:
                dst[:, cols] = value
            else:
                dst[dst_rows, cols] = value
            return carry
        lax.fori_loop(0, total // TILE, one, 0)

    top_half, low_half = pl.ds(0, tok), pl.ds(tok, tok)
    rs_keys = ((1, 0), (1, 1), (2, 0), (2, 1), (3, 0), (3, 1))

    def scatter_send(name, k, h, dst, target):
        rows_of = (top_half, low_half)[h]
        remote(s.fs.at[k, rows_of], dst.at[rows_of], (name, k, h), (name, k, h), dev(c, z, plane_peers[target]))

    def plane_scatter_chunk(k, fn, name):
        if k == 0:
            column_tiles(fn, model, s.own)
            return
        column_tiles(fn, model, s.fs.at[k])
        scatter_start(k, name)

    def scatter_start(k, name):
        if k == 1:
            scatter_send(name, 1, 0, s.fr.at[1], 1)
        if k == 2:
            scatter_send(name, 2, 1, s.fr.at[2], 2)
        if k == 3:
            scatter_send(name, 3, 0, s.fr.at[0], 1)
            scatter_send(name, 3, 1, s.fr.at[0], 2)

    def plane_scatter_pass(name):
        for h, k in ((0, 2), (1, 1)):
            rows_of = (top_half, low_half)[h]
            arrived(s.fr.at[0, rows_of], (name, 3, h))
            s.fs[k, rows_of, :] = (
                s.fs[k, rows_of, :].astype(F32) + s.fr[0, rows_of, :].astype(F32)
            ).astype(BF16)
            scatter_send(name, k, h, s.fr.at[k], k)

    def plane_scatter_sum(name):
        for k in (1, 2):
            for h in (0, 1):
                arrived(s.fr.at[k, top_half], (name, k, h))
        return s.own[...] + s.fr[1].astype(F32) + s.fr[2].astype(F32)

    def plane_sent_now(name):
        for k, h in rs_keys:
            ref = s.fs.at[k, top_half]
            pltpu.make_async_copy(ref, ref, sem(SEND, (name, k, h))).wait()

    def chunk_rows(k):
        return wide_slice(plane_peers[k] * chunk, chunk, chunk)

    for k in range(4):
        here = chunk_rows(k)
        hid_gather.done(k)
        ffn_first(here)
        if k == 0:
            hid_gather.step1()
            wf.step2()
    wf.step3()
    wf.done()
    for k in (3, 1, 2, 0):
        here = chunk_rows(k)
        plane_scatter_chunk(k, lambda cols: mm(s.act[here, :], s.wfo[:, cols]), N.rs1)
    plane_scatter_pass(N.rs1)

    branch = plane_scatter_sum(N.rs1) + row_vec(5)
    normed2, inverse2 = normalize_rows(s.aft[...] + branch)
    gain2 = row_vec(6)
    s.outl[...] = (normed2 * gain2 + row_vec(7)).astype(BF16)
    arrived(s.cin, N.c)
    upstream = s.cin[...].astype(F32)
    s.smg[...] = jnp.zeros_like(s.smg)
    s.smg[6:7, :] = jnp.sum(upstream * normed2, axis=0, keepdims=True)
    s.smg[7:8, :] = jnp.sum(upstream, axis=0, keepdims=True)

    def norm_back(up, normed_rows, inverse_rows, gain):
        scaled = up * gain
        return inverse_rows * (
            scaled
            - jnp.mean(scaled, axis=-1, keepdims=True)
            - normed_rows * jnp.mean(scaled * normed_rows, axis=-1, keepdims=True)
        )

    second = norm_back(upstream, normed2, inverse2, gain2)
    s.second[...] = second
    second_low = second.astype(BF16)
    s.bg[own_rows, :] = second_low
    bg_gather = plane_gather(s.bg, N.bg)
    s.smg[5:6, :] = jnp.sum(second_low.astype(F32), axis=0, keepdims=True)

    def send_home(src, dst, name):
        for i in range(2):
            is_self = jnp.logical_and(home == c, 2 * c + i == z)
            maybe_local(
                src.at[pl.ds(i * tok, tok)], dst.at[slot], (name, i), name,
                dev(home, 2 * c + i, p), is_self,
            )

    send_home(s.outl, s.outr, N.out)

    def ffn_back(here):
        def one(n, carry):
            cols = wide_slice(n * TILE, TILE, TILE)
            acc = mm(s.bg[here, :], s.wfo[cols, :], 1, 1)
            s.pg[here, cols] = (acc * s.pre[here, cols]).astype(BF16)
            return carry
        lax.fori_loop(0, units // TILE, one, 0)

    def grad_sibling(lhs, rhs, buf_s, name):
        def one(m, carry):
            at = wide_slice(m * TILE, TILE, TILE)
            cols = wide_slice(other * half + m * TILE, TILE, TILE)
            buf_s[at, :] = mm(lhs[:, cols], rhs[...], 0, 0).astype(BF16)
            return carry
        lax.fori_loop(0, half // TILE, one, 0)

    def sibling_send(buf_s, buf_r, name):
        remote(buf_s, buf_r, name, name, dev(other, z, p))
        sent(buf_s, name)

    def grad_own(lhs, rhs, buf_r, scatter, name):
        arrived(buf_r, name)
        for k in (2, 3, 1, 0):
            at = wide_slice(z_peers[k] * zrows, zrows, zrows)
            cols = wide_slice(c * half + z_peers[k] * zrows, zrows, zrows)
            value = mm(lhs[:, cols], rhs[...], 0, 0) + buf_r[at, :].astype(F32)
            if k:
                scatter.part[z_peers[k]] = value.astype(BF16)
            else:
                scatter.keep[...] = value
        scatter.step0()

    gfo = ZScatter((N.gfo, N.z), s.gfo_zs, s.gfo_o, s.gfo_zr)
    gwi = ZScatter((N.gwi, N.z), s.gwi_zs, s.gwi_o, s.gwi_zr)
    gqk = ZScatter((N.gqk, N.z), s.gqk_zs, s.gqk_o, s.gqk_zr)
    gwo = ZScatter((N.gwo, N.z), s.gwo_zs, s.gwo_t, s.gwo_zr)

    plane_sent_now(N.rs1)

    def hidden_chunk(k):
        here = chunk_rows(k)
        plane_scatter_chunk(k, lambda cols: mm(s.pg[here, :], s.win[cols, :], 1, 1), N.rs2)

    for k in range(4):
        bg_gather.done(k)
        if k == 3:
            grad_sibling(s.act, s.bg, s.gfo_s, N.gfo)
            sibling_send(s.gfo_s, s.gfo_r, N.gfo)
        ffn_back(chunk_rows(k))
        if k == 0:
            bg_gather.step1()
        else:
            hidden_chunk(k)
    grad_own(s.act, s.bg, s.gfo_r, gfo, N.gfo)
    plane_scatter_pass(N.rs2)
    grad_sibling(s.hid, s.pg, s.gwi_s, N.gwi)
    sibling_send(s.gwi_s, s.gwi_r, N.gwi)
    hidden_chunk(0)
    s.smg[8:9, :] = jnp.sum(s.pg[...].astype(F32), axis=0, keepdims=True)
    grad_own(s.hid, s.pg, s.gwi_r, gwi, N.gwi)

    hidden_grad = s.second[...] + plane_scatter_sum(N.rs2)
    normed = s.n1[...]
    s.smg[3:4, :] = jnp.sum(hidden_grad * normed, axis=0, keepdims=True)
    s.smg[4:5, :] = jnp.sum(hidden_grad, axis=0, keepdims=True)
    first = norm_back(hidden_grad, normed, s.inv1[...], row_vec(3))
    s.first[...] = first
    first_low = first.astype(BF16)
    s.agl[...] = first_low
    s.smg[2:3, :] = jnp.sum(first_low.astype(F32), axis=0, keepdims=True)
    column_tiles(lambda cols: mm(s.agl[...], s.wo[cols, :], 1, 1), model, s.ado)
    for k in (1, 2, 3):
        pp = plane_peers[k]
        remote(
            s.ado.at[:, wide_slice(pp * wid, wid, wid)],
            s.do.at[own_rows],
            N.do, (N.do, k), dev(c, z, pp),
        )
    sent(s.do.at[pl.ds(0, 3 * chunk)], N.do)
    s.do[own_rows, :] = s.ado[:, wide_slice(p * wid, wid, wid)]

    grad_sibling(s.attx, s.agl, s.gwo_s, N.gwo)
    sibling_send(s.gwo_s, s.gwo_r, N.gwo)

    for k in (1, 2, 3):
        arrived(s.do.at[pl.ds(0, chunk)], (N.do, k))

    s.dq[...] = jnp.zeros_like(s.dq)
    s.dk[...] = jnp.zeros_like(s.dk)
    s.dv[...] = jnp.zeros_like(s.dv)

    def attend_back(step, carry):
        h = step % heads
        t = step // heads
        here = wide_slice(t * qt, qt, qt)
        mask = head_mask(h, qt)
        queries = jnp.where(mask, s.q[here, :].astype(F32) * scale, 0.0).astype(BF16)
        scores = mm(queries, s.kv[:, 0:wid], 1, 1) + s.bias[here, :]
        probs = jnp.exp(scores - s.lse[h, here, :])
        grads = jnp.where(mask, s.do[here, :].astype(F32), 0.0)
        residue = jnp.sum(grads * s.att[here, :], axis=-1, keepdims=True)
        grads = grads.astype(BF16)
        prob_grad = mm(grads, s.kv[:, wid:2 * wid], 1, 1)
        score_grad = (probs * (prob_grad - residue)).astype(BF16)
        s.dv[...] += mm(probs.astype(BF16), grads, 0, 0)
        s.dk[...] += mm(score_grad, queries, 0, 0)
        s.dq[here, :] += jnp.where(mask, mm(score_grad, s.kv[:, 0:wid]), 0.0)
        return carry

    lax.fori_loop(0, steps // 4, attend_back, 0)
    arrived(s.gwo_r, N.gwo)

    def own_tile(m, carry):
        at = wide_slice(m * TILE, TILE, TILE)
        cols = wide_slice(c * half + m * TILE, TILE, TILE)
        value = mm(s.attx[:, cols], s.agl[...], 0, 0) + s.gwo_r[at, :].astype(F32)
        s.gwo_o[at, :] = value
        s.gwo_p[at, :] = value.astype(BF16)
        return carry

    lax.fori_loop(0, half // TILE, own_tile, 0)

    for k in (1, 2, 3):
        for zz in range(PLANES):
            remote(
                s.gwo_p.at[wide_slice(zz * zrows + plane_peers[k] * rows, rows, rows)],
                s.gwo_pr.at[k, zz],
                N.gwop, (N.gwop, k), dev(c, z, plane_peers[k]),
            )
    sent(s.gwo_p.at[pl.ds(0, 3 * PLANES * rows)], N.gwop)
    gfo.step1()
    lax.fori_loop(steps // 4, steps, attend_back, 0)
    gfo.step2()
    theirs = wide_slice(other * toks, toks, toks)
    mine = wide_slice(c * toks, toks, toks)
    s.dkvs[:, 0:wid] = s.dk[theirs, :].astype(BF16)
    s.dkvs[:, wid:2 * wid] = s.dv[theirs, :].astype(BF16)
    sibling_send(s.dkvs, s.dkvr, N.dkv)
    s.dqkv[:, 0:wid] = (s.dq[...] * scale).astype(BF16)

    arrived(s.dkvr, N.dkv)
    s.dqkv[:, wid:2 * wid] = (s.dk[mine, :] + s.dkvr[:, 0:wid].astype(F32)).astype(BF16)
    s.dqkv[:, 2 * wid:3 * wid] = (s.dv[mine, :] + s.dkvr[:, wid:2 * wid].astype(F32)).astype(BF16)

    plane_sent_now(N.rs2)
    for k in (3, 1, 2, 0):
        here = chunk_rows(k)
        plane_scatter_chunk(k, lambda cols: mm(s.dqkv[here, :], s.wqkv[cols, :], 1, 1), N.rs3)

    grad_sibling(s.slow, s.dqkv, s.gqk_s, N.gqk)
    sibling_send(s.gqk_s, s.gqk_r, N.gqk)
    plane_scatter_pass(N.rs3)
    gwi.step1()
    grad_own(s.slow, s.dqkv, s.gqk_r, gqk, N.gqk)
    gwi.step2()

    low_sum = jnp.sum(s.dqkv[...].astype(F32), axis=0, keepdims=True)
    pcols = wide_slice(p * wid, wid, wid)
    s.smg[0:1, pcols] = low_sum[:, 0:wid]
    s.smg[1:2, pcols] = low_sum[:, 2 * wid:3 * wid]
    for cc in range(2):
        for k in range(4):
            if cc == 0 and k == 0:
                continue
            tc = other if cc else c
            lanes = wide_slice((tc * 4 + z_peers[k]) * 128, 128, 128)
            remote(s.smg.at[:, lanes], s.sma.at[cc * 4 + k], N.sma, (N.sma, cc, k), dev(tc, z_peers[k], p))
    sent(s.smg.at[:, pl.ds(0, 7 * 128)], N.sma)

    total = s.first[...] + plane_scatter_sum(N.rs3)
    s.igl[...] = total.astype(BF16)
    send_home(s.igl, s.igr, N.ig)

    for k in (1, 2, 3):
        arrived(s.gwo_pr.at[k], (N.gwop, k))

    def gwo_total(zz):
        value = s.gwo_o[wide_slice(zz * zrows + p * rows, rows, rows), :]
        for k in (1, 2, 3):
            value = value + s.gwo_pr[k, zz].astype(F32)
        return value

    for k in (2, 3, 1):
        s.gwo_zs[z_peers[k]] = gwo_total(z_peers[k]).astype(BF16)
    s.gwo_t[...] = gwo_total(z)
    gwo.step0()

    gwi.step3()

    def plane_rows(buf_p, buf_pr, name):
        for k in (1, 2, 3):
            remote(
                buf_p.at[wide_slice(plane_peers[k] * rows, rows, rows)], buf_pr.at[k],
                name, (name, k), dev(c, z, plane_peers[k]),
            )
        sent(buf_p.at[pl.ds(0, 3 * rows)], name)

    s.gwi_p[...] = s.gwi_o[...].astype(BF16)
    plane_rows(s.gwi_p, s.gwi_pr, N.gwip)
    gfo.step3()
    dwfo_ref[...] = s.gfo_o[...]
    gqk.step1()
    gwo.step1()

    def dwin_piece(k):
        if k:
            arrived(s.gwi_pr.at[k], (N.gwip, k))
        pp = plane_peers[k]
        for g in range(8):
            piece_cols = slice(g * frows, (g + 1) * frows)
            if k:
                value = s.gwi_pr[k, :, piece_cols].astype(F32)
            else:
                value = s.gwi_o[wide_slice(p * rows, rows, rows), piece_cols]
            dwin_ref[:, wide_slice(g * 4 * frows + pp * frows, frows, frows)] = value

    part = s.smg[:, wide_slice((c * 4 + z) * 128, 128, 128)]
    for cc in range(2):
        for k in range(4):
            if cc == 0 and k == 0:
                continue
            arrived(s.sma.at[cc * 4 + k], (N.sma, cc, k))
            part = part + s.sma[cc * 4 + k]
    s.smb[...] = part
    for k in (1, 2, 3):
        remote(s.smb, s.smb_r.at[k], N.smb, (N.smb, k), dev(c, z, plane_peers[k]))
    sent(s.smb_r.at[pl.ds(0, 3)], N.smb)

    gqk.step2()
    gwo.step2()
    arrived(s.outr, N.out)
    out_ref[...] = s.outr[...]
    for k in range(4):
        dwin_piece(k)
    gqk.step3()
    s.gqk_p[...] = s.gqk_o[...].astype(BF16)
    plane_rows(s.gqk_p, s.gqk_pr, N.gqkp)

    gwo.step3()
    dwo_ref[...] = s.gwo_t[...]
    all_rows = s.smb[...]
    for k in (1, 2, 3):
        arrived(s.smb_r.at[k], (N.smb, k))
        all_rows = all_rows + s.smb_r[k]
    row_ids = lax.broadcasted_iota(jnp.int32, (16, 128), 0)
    sg_ref[...] = jnp.where(row_ids == 8, s.smb[...], all_rows)
    for k in range(4):
        if k:
            arrived(s.gqk_pr.at[k], (N.gqkp, k))
        pp = plane_peers[k]
        for t in range(3):
            piece_cols = slice(t * wid, (t + 1) * wid)
            if k:
                value = s.gqk_pr[k, :, piece_cols].astype(F32)
            else:
                value = s.gqk_o[wide_slice(p * rows, rows, rows), piece_cols]
            dwqkv_ref[:, wide_slice(t * model + pp * wid, wid, wid)] = value
    arrived(s.igr, N.ig)
    ig_ref[...] = s.igr[...]

    @pl.when(table_here)
    def _():
        handle = sem(SEND, N.tbl)
        pltpu.make_async_copy(s.tbl, s.tbl, handle).wait()

    plane_sent_now(N.rs3)
    flush_sent()


def fused_local(
    inputs, segments, pad_mask, timesteps, w_qkv, bias_query, bias_value, w_attn_out, bias_attn_out,
    ln1_gain, ln1_shift, w_ffn_in, bias_ffn_in, w_ffn_out, bias_ffn_out, ln2_gain, ln2_shift, cotangent,
):
    _, tok, model = inputs.shape
    hidden = w_ffn_in.shape[1]
    rows = w_qkv.shape[0]
    blk = lax.axis_index("blk")
    half_width = model // 2
    frequency = jnp.exp(
        jnp.arange(half_width, dtype=F32) * (-math.log(10000.0) / half_width)
    )
    angles = timesteps.astype(F32)[..., None] * (100.0 / TSTEPS) * frequency
    table = jnp.concatenate([jnp.sin(angles), jnp.cos(angles)], axis=-1)
    vectors = jnp.stack(
        [bias_query, bias_value, bias_attn_out, ln1_gain, ln1_shift, bias_ffn_out, ln2_gain, ln2_shift]
    )
    small = jnp.concatenate(
        [
            jnp.pad(vectors, ((0, 0), (0, 128 - rows))),
            bias_ffn_in[None],
            jnp.zeros((7, 128), BF16),
        ]
    )
    codes = jnp.where(pad_mask == 1, segments, -1)
    marks = jnp.stack([segments, codes], axis=1).astype(F32) + 1.0
    odd = (blk // PLANE) % 2 == 1
    marks = jnp.concatenate([jnp.where(odd, 0.0, marks), jnp.where(odd, marks, 0.0)], axis=-1)
    info = jnp.pad(marks, ((0, 0), (0, 6), (0, 0)))

    plan = scratch_plan(tok, model, hidden)
    vmem = pl.BlockSpec(memory_space=pltpu.VMEM)
    outs = pl.pallas_call(
        functools.partial(fused, plan, tok, model, hidden),
        out_shape=(
            jax.ShapeDtypeStruct((2, tok, model), BF16),
            jax.ShapeDtypeStruct((2, tok, model), BF16),
            jax.ShapeDtypeStruct((rows, 3 * model), F32),
            jax.ShapeDtypeStruct((rows, model), F32),
            jax.ShapeDtypeStruct((rows, hidden), F32),
            jax.ShapeDtypeStruct((hidden // 32, model), F32),
            jax.ShapeDtypeStruct((16, 128), F32),
        ),
        in_specs=[vmem] * 9,
        out_specs=[vmem] * 7,
        scratch_shapes=[pltpu.VMEM(shape, dtype) for shape, dtype in plan.values()]
        + [pltpu.SemaphoreType.DMA((N_SEND,)), pltpu.SemaphoreType.DMA((N_RECV,))],
        compiler_params=pltpu.CompilerParams(
            collective_id=0, has_side_effects=True, vmem_limit_bytes=63 * 1024 * 1024
        ),
    )(inputs, cotangent, table, small, info, w_qkv, w_attn_out, w_ffn_in, w_ffn_out)
    out, input_grad, g_qkv, g_out, g_in, g_down, g_small = outs
    mine = lax.dynamic_slice(g_small, (0, (blk % PLANE) * rows), (8, rows))
    return (
        out, input_grad, g_qkv, mine[0], mine[1], g_out, mine[2], mine[3], mine[4],
        g_in, g_small[8], g_down, mine[5], mine[6], mine[7],
    )


def layer(*args):
    inputs, w_qkv, w_ffn_out = args[0], args[4], args[13]
    fits = (
        lax.axis_size("dp") == 2
        and lax.axis_size("blk") == PLANE * PLANES
        and inputs.shape[0] == 2
        and inputs.shape[1] == 64
        and w_qkv.shape[0] * PLANE == 128
        and w_ffn_out.shape[0] == 128
        and args[3].shape[1] <= 8
    )
    return (fused_local if fits else local)(*args)


def solution(mesh):
    return jax.shard_map(
        layer,
        mesh=mesh,
        in_specs=(
            P("dp", "blk", None),
            P("dp", "blk"),
            P("dp", "blk"),
            P("dp", None),
            P(("dp", "blk"), None),
            P(("dp", "blk")),
            P(("dp", "blk")),
            P(("dp", "blk"), None),
            P(("dp", "blk")),
            P(("dp", "blk")),
            P(("dp", "blk")),
            P(("dp", "blk"), None),
            P(("dp", "blk")),
            P(("dp", "blk"), None),
            P(("dp", "blk")),
            P(("dp", "blk")),
            P(("dp", "blk")),
            P("dp", "blk", None),
        ),
        out_specs=(
            P("dp", "blk", None),
            P("dp", "blk", None),
            P(("dp", "blk"), None),
            P(("dp", "blk")),
            P(("dp", "blk")),
            P(("dp", "blk"), None),
            P(("dp", "blk")),
            P(("dp", "blk")),
            P(("dp", "blk")),
            P(("dp", "blk"), None),
            P(("dp", "blk")),
            P(("dp", "blk"), None),
            P(("dp", "blk")),
            P(("dp", "blk")),
            P(("dp", "blk")),
        ),
        check_vma=False,
    )
```

```python
import functools
import math

import jax
import jax.numpy as jnp
from jax import lax
from jax.experimental import pallas as pl
from jax.experimental.pallas import tpu as pltpu
from jax.sharding import PartitionSpec as P

HEADS = 16
HEAD = 64
TSTEPS = 5000


EPSILON = 1e-05
NEGATIVE = -1e30


def time_features(timesteps, segments, model_width):
    item_count = timesteps.shape[1]
    numbers = jnp.arange(item_count, dtype=jnp.int32)
    picked = jnp.sum(
        jnp.where(segments[:, :, None] == numbers[None, None, :], timesteps[:, None, :], 0), axis=-1
    )
    half_width = model_width // 2
    frequency = jnp.exp(
        jnp.arange(half_width, dtype=jnp.float32) * (-math.log(10000.0) / half_width)
    )
    angles = picked.astype(jnp.float32)[..., None] * (100.0 / TSTEPS) * frequency
    return jnp.concatenate([jnp.sin(angles), jnp.cos(angles)], axis=-1)


def normalize(hidden):
    centered = hidden - jnp.mean(hidden, axis=-1, keepdims=True)
    inverse = lax.rsqrt(jnp.mean(centered * centered, axis=-1, keepdims=True) + EPSILON)
    return (centered * inverse, inverse)


def norm_backward(upstream, normed, inverse, gain):
    scaled = upstream * gain
    return inverse * (
        scaled
        - jnp.mean(scaled, axis=-1, keepdims=True)
        - normed * jnp.mean(scaled * normed, axis=-1, keepdims=True)
    )


def exact_gelu(values):
    return jax.nn.gelu(values, approximate=False)


def local(
    inputs,
    segments,
    pad_mask,
    timesteps,
    w_qkv,
    bias_query,
    bias_value,
    w_attn_out,
    bias_attn_out,
    ln1_gain,
    ln1_shift,
    w_ffn_in,
    bias_ffn_in,
    w_ffn_out,
    bias_ffn_out,
    ln2_gain,
    ln2_shift,
    cotangent,
):
    row_count, tok_count, model_width = inputs.shape
    flat_count = row_count * tok_count
    head_count = HEADS
    head_dim = HEAD
    scale = HEAD ** (-0.5)
    bf16 = jnp.bfloat16
    single = jnp.float32
    attn_full = (
        lax.all_gather(w_qkv, ("dp", "blk"), axis=0, tiled=True),
        lax.all_gather(bias_query, ("dp", "blk"), axis=0, tiled=True),
        lax.all_gather(bias_value, ("dp", "blk"), axis=0, tiled=True),
        lax.all_gather(w_attn_out, ("dp", "blk"), axis=0, tiled=True),
        lax.all_gather(bias_attn_out, ("dp", "blk"), axis=0, tiled=True),
        lax.all_gather(ln1_gain, ("dp", "blk"), axis=0, tiled=True),
        lax.all_gather(ln1_shift, ("dp", "blk"), axis=0, tiled=True),
    )
    qkv_weight, query_bias, value_bias, out_weight, out_bias, gain_one, shift_one = attn_full
    embedded = time_features(timesteps, segments, model_width)
    start_flat = (inputs.astype(single) + embedded).reshape(flat_count, model_width)
    start_low = start_flat.astype(bf16)
    projected = jnp.dot(start_low, qkv_weight, preferred_element_type=single)
    query_send = (
        (projected[:, :model_width] + query_bias.astype(single))
        .astype(bf16)
        .reshape(row_count, tok_count, model_width)
    )
    key_send = (
        projected[:, model_width : 2 * model_width]
        .astype(bf16)
        .reshape(row_count, tok_count, model_width)
    )
    value_send = (
        (projected[:, 2 * model_width :] + value_bias.astype(single))
        .astype(bf16)
        .reshape(row_count, tok_count, model_width)
    )
    query_heads = query_send.reshape(row_count, tok_count, head_count, head_dim)
    key_heads = key_send.reshape(row_count, tok_count, head_count, head_dim)
    value_heads = value_send.reshape(row_count, tok_count, head_count, head_dim)
    codes = jnp.where(pad_mask == 1, segments, -1)
    code_float = codes.astype(single)
    seg_float = segments.astype(single)
    code_send = codes.astype(bf16)
    seg_send = segments.astype(bf16)

    def split_heads(piece):
        return piece.reshape(piece.shape[0], piece.shape[1], head_count, head_dim)

    piece = (
        lax.all_gather(key_send, "blk", axis=1, tiled=True),
        lax.all_gather(value_send, "blk", axis=1, tiled=True),
        lax.all_gather(code_send, "blk", axis=1, tiled=True),
    )
    run_max = jnp.full((row_count, tok_count, head_count), NEGATIVE, single)
    piece_keys = split_heads(piece[0])
    piece_values = split_heads(piece[1])
    scores = (
        jnp.einsum("rqhe,rkhe->rqhk", query_heads, piece_keys, preferred_element_type=single)
        * scale
    )
    valid = seg_float[:, :, None, None] == piece[2].astype(single)[:, None, None, :]
    masked = jnp.where(valid, scores, NEGATIVE)
    new_max = jnp.maximum(run_max, jnp.max(masked, axis=-1))
    weights = jnp.where(valid, jnp.exp(masked - new_max[..., None]), 0.0)
    run_sum = jnp.sum(weights, axis=-1)
    run_acc = jnp.einsum(
        "rqhk,rkhe->rqhe", weights.astype(bf16), piece_values, preferred_element_type=single
    )
    run_max, run_sum, run_acc = (new_max, run_sum, run_acc)
    log_total = run_max + jnp.log(run_sum)
    attended = run_acc / run_sum[..., None]
    attended_low = attended.reshape(flat_count, model_width).astype(bf16)
    attn_branch = jnp.dot(
        attended_low, out_weight, preferred_element_type=single
    ) + out_bias.astype(single)
    normed_one, inverse_one = normalize(start_flat + attn_branch)
    gain_one_f = gain_one.astype(single)
    after_attn = normed_one * gain_one_f + shift_one.astype(single)
    ffn_full = (
        lax.all_gather(w_ffn_in, ("dp", "blk"), axis=0, tiled=True),
        lax.all_gather(bias_ffn_in, ("dp", "blk"), axis=0, tiled=True),
        lax.all_gather(w_ffn_out, ("dp", "blk"), axis=0, tiled=True),
        lax.all_gather(bias_ffn_out, ("dp", "blk"), axis=0, tiled=True),
        lax.all_gather(ln2_gain, ("dp", "blk"), axis=0, tiled=True),
        lax.all_gather(ln2_shift, ("dp", "blk"), axis=0, tiled=True),
    )
    in_weight, in_bias, down_weight, down_bias, gain_two, shift_two = ffn_full
    hidden_low = after_attn.astype(bf16)
    pre_act = jnp.dot(hidden_low, in_weight, preferred_element_type=single) + in_bias.astype(single)
    activated, gelu_pull = jax.vjp(exact_gelu, pre_act)
    activated_low = activated.astype(bf16)
    branch = jnp.dot(activated_low, down_weight, preferred_element_type=single) + down_bias.astype(
        single
    )
    normed_two, inverse_two = normalize(after_attn + branch)
    gain_two_f = gain_two.astype(single)
    outputs = (
        (normed_two * gain_two_f + shift_two.astype(single))
        .astype(bf16)
        .reshape(row_count, tok_count, model_width)
    )
    ffn_back = (
        lax.all_gather(w_ffn_in, ("dp", "blk"), axis=0, tiled=True),
        lax.all_gather(w_ffn_out, ("dp", "blk"), axis=0, tiled=True),
    )
    in_weight_back, down_weight_back = ffn_back
    upstream = cotangent.astype(single).reshape(flat_count, model_width)
    gain_two_grad = jnp.sum(upstream * normed_two, axis=0)
    shift_two_grad = jnp.sum(upstream, axis=0)
    second_grad = norm_backward(upstream, normed_two, inverse_two, gain_two_f)
    branch_grad = second_grad.astype(bf16)
    down_weight_grad = jnp.einsum(
        "tf,td->fd", activated_low, branch_grad, preferred_element_type=single
    )
    down_bias_grad = jnp.sum(branch_grad.astype(single), axis=0)
    act_grad = jnp.einsum("td,fd->tf", branch_grad, down_weight_back, preferred_element_type=single)
    pre_grad = gelu_pull(act_grad)[0].astype(bf16)
    in_weight_grad = jnp.einsum("td,tf->df", hidden_low, pre_grad, preferred_element_type=single)
    in_bias_grad = jnp.sum(pre_grad.astype(single), axis=0)
    hidden_grad = second_grad + jnp.einsum(
        "tf,df->td", pre_grad, in_weight_back, preferred_element_type=single
    )
    gain_one_grad = jnp.sum(hidden_grad * normed_one, axis=0)
    shift_one_grad = jnp.sum(hidden_grad, axis=0)
    first_grad = norm_backward(hidden_grad, normed_one, inverse_one, gain_one_f)
    ffn_grads = (
        lax.psum_scatter(in_weight_grad, ("dp", "blk"), scatter_dimension=0, tiled=True),
        lax.psum_scatter(in_bias_grad, ("dp", "blk"), scatter_dimension=0, tiled=True),
        lax.psum_scatter(down_weight_grad, ("dp", "blk"), scatter_dimension=0, tiled=True),
        lax.psum_scatter(down_bias_grad, ("dp", "blk"), scatter_dimension=0, tiled=True),
        lax.psum_scatter(gain_two_grad, ("dp", "blk"), scatter_dimension=0, tiled=True),
        lax.psum_scatter(shift_two_grad, ("dp", "blk"), scatter_dimension=0, tiled=True),
    )
    attn_back = (
        lax.all_gather(w_qkv, ("dp", "blk"), axis=0, tiled=True),
        lax.all_gather(w_attn_out, ("dp", "blk"), axis=0, tiled=True),
    )
    qkv_weight_back, out_weight_back = attn_back
    attn_grad_low = first_grad.astype(bf16)
    out_weight_grad = jnp.einsum(
        "td,te->de", attended_low, attn_grad_low, preferred_element_type=single
    )
    out_bias_grad = jnp.sum(attn_grad_low.astype(single), axis=0)
    attended_grad = jnp.einsum(
        "te,de->td", attn_grad_low, out_weight_back, preferred_element_type=single
    ).astype(bf16)
    grad_send = attended_grad.reshape(row_count, tok_count, model_width)
    grad_heads = grad_send.reshape(row_count, tok_count, head_count, head_dim)
    residue = jnp.sum(grad_heads.astype(single) * attended, axis=-1)
    stats_full = (
        lax.all_gather(log_total, "blk", axis=1, tiled=True),
        lax.all_gather(residue, "blk", axis=1, tiled=True),
    )
    log_full, residue_full = stats_full
    piece = (
        lax.all_gather(key_send, "blk", axis=1, tiled=True),
        lax.all_gather(value_send, "blk", axis=1, tiled=True),
        lax.all_gather(code_send, "blk", axis=1, tiled=True),
    )
    piece_keys = split_heads(piece[0])
    piece_values = split_heads(piece[1])
    scores = (
        jnp.einsum("rqhe,rkhe->rqhk", query_heads, piece_keys, preferred_element_type=single)
        * scale
    )
    valid = seg_float[:, :, None, None] == piece[2].astype(single)[:, None, None, :]
    probs = jnp.exp(jnp.where(valid, scores - log_total[..., None], NEGATIVE))
    prob_grad = jnp.einsum(
        "rqhe,rkhe->rqhk", grad_heads, piece_values, preferred_element_type=single
    )
    score_grad = (probs * (prob_grad - residue[..., None])).astype(bf16)
    query_grad = (
        jnp.einsum("rqhk,rkhe->rqhe", score_grad, piece_keys, preferred_element_type=single) * scale
    )
    piece = (
        lax.all_gather(query_send, "blk", axis=1, tiled=True),
        lax.all_gather(grad_send, "blk", axis=1, tiled=True),
        lax.all_gather(seg_send, "blk", axis=1, tiled=True),
    )
    piece_queries = split_heads(piece[0])
    piece_grads = split_heads(piece[1])
    scores = (
        jnp.einsum("rqhe,rkhe->rqhk", piece_queries, key_heads, preferred_element_type=single)
        * scale
    )
    valid = piece[2].astype(single)[:, :, None, None] == code_float[:, None, None, :]
    probs = jnp.exp(jnp.where(valid, scores - log_full[..., None], NEGATIVE))
    value_acc = jnp.einsum(
        "rqhk,rqhe->rkhe", probs.astype(bf16), piece_grads, preferred_element_type=single
    )
    prob_grad = jnp.einsum(
        "rqhe,rkhe->rqhk", piece_grads, value_heads, preferred_element_type=single
    )
    score_grad = (probs * (prob_grad - residue_full[..., None])).astype(bf16)
    key_acc = (
        jnp.einsum("rqhk,rqhe->rkhe", score_grad, piece_queries, preferred_element_type=single)
        * scale
    )
    query_low = query_grad.astype(bf16).reshape(flat_count, model_width)
    key_low = key_acc.astype(bf16).reshape(flat_count, model_width)
    value_low = value_acc.astype(bf16).reshape(flat_count, model_width)
    qkv_grad = jnp.concatenate([query_low, key_low, value_low], axis=1)
    qkv_weight_grad = jnp.einsum("td,tc->dc", start_low, qkv_grad, preferred_element_type=single)
    query_bias_grad = jnp.sum(query_low.astype(single), axis=0)
    value_bias_grad = jnp.sum(value_low.astype(single), axis=0)
    input_grad = (
        first_grad
        + jnp.einsum("tc,dc->td", qkv_grad, qkv_weight_back, preferred_element_type=single)
    ).astype(bf16)
    input_grad = input_grad.reshape(row_count, tok_count, model_width)
    attn_grads = (
        lax.psum_scatter(qkv_weight_grad, ("dp", "blk"), scatter_dimension=0, tiled=True),
        lax.psum_scatter(query_bias_grad, ("dp", "blk"), scatter_dimension=0, tiled=True),
        lax.psum_scatter(value_bias_grad, ("dp", "blk"), scatter_dimension=0, tiled=True),
        lax.psum_scatter(out_weight_grad, ("dp", "blk"), scatter_dimension=0, tiled=True),
        lax.psum_scatter(out_bias_grad, ("dp", "blk"), scatter_dimension=0, tiled=True),
        lax.psum_scatter(gain_one_grad, ("dp", "blk"), scatter_dimension=0, tiled=True),
        lax.psum_scatter(shift_one_grad, ("dp", "blk"), scatter_dimension=0, tiled=True),
    )
    return (
        outputs,
        input_grad,
        attn_grads[0],
        attn_grads[1],
        attn_grads[2],
        attn_grads[3],
        attn_grads[4],
        attn_grads[5],
        attn_grads[6],
        ffn_grads[0],
        ffn_grads[1],
        ffn_grads[2],
        ffn_grads[3],
        ffn_grads[4],
        ffn_grads[5],
    )


MESH = pl.DeviceIdType.MESH
PLANE = 4
PLANES = 4
TILE = 256
BF16 = jnp.bfloat16
F32 = jnp.float32


def mm(left, right, left_dim=1, right_dim=0):
    return lax.dot_general(
        left, right, (((left_dim,), (right_dim,)), ((), ())), preferred_element_type=F32
    )


def wide_slice(start, size, step):
    return pl.ds(pl.multiple_of(start, step), size)


class Names:
    pass


class Labels:
    def __getattr__(self, name):
        return name


N = Labels()
SEND, RECV = 0, 1


def scratch_plan(tok, model, hidden):
    chunk = 2 * tok
    toks = PLANE * chunk
    keys = 2 * toks
    wid = model // PLANE
    units = hidden // PLANE
    rows = model // 32
    zrows = PLANE * rows
    half = PLANES * zrows
    return dict(
        xin=((chunk, model), BF16),
        cin=((chunk, model), BF16),
        tbl=((8, model), F32),
        inf_in=((2, 8, 128), F32),
        inf=((8, 8, 128), F32),
        smalls=((2, PLANES, PLANE, 16, 128), BF16),
        vec=((16, model), F32),
        ffb=((16, units), F32),
        wqkv=((model, 3 * wid), BF16),
        wo=((model, model), BF16),
        win=((model, units), BF16),
        wfo=((units, model), BF16),
        sres=((chunk, model), F32),
        slow=((toks, model), BF16),
        q=((toks, wid), BF16),
        kv=((keys, 2 * wid), BF16),
        bias=((toks, keys), F32),
        att=((toks, wid), F32),
        lse=((4, toks, 1), F32),
        attl=((toks, wid), BF16),
        attx=((chunk, model), BF16),
        n1=((chunk, model), F32),
        inv1=((chunk, 1), F32),
        aft=((chunk, model), F32),
        hid=((toks, model), BF16),
        pre=((toks, units), F32),
        act=((toks, units), BF16),
        fs=((PLANE, chunk, model), BF16),
        fr=((3, chunk, model), BF16),
        own=((chunk, model), F32),
        outl=((chunk, model), BF16),
        outr=((2, tok, model), BF16),
        second=((chunk, model), F32),
        bg=((toks, model), BF16),
        pg=((toks, units), BF16),
        first=((chunk, model), F32),
        agl=((chunk, model), BF16),
        ado=((chunk, model), BF16),
        do=((toks, wid), BF16),
        dq=((toks, wid), F32),
        dk=((keys, wid), F32),
        dv=((keys, wid), F32),
        dkvs=((toks, 2 * wid), BF16),
        dkvr=((toks, 2 * wid), BF16),
        dqkv=((toks, 3 * wid), BF16),
        igl=((chunk, model), BF16),
        igr=((2, tok, model), BF16),
        gfo_s=((half, model), BF16),
        gfo_r=((half, model), BF16),
        gfo_o=((zrows, model), F32),
        gfo_zs=((4, zrows, model), BF16),
        gfo_zr=((5, zrows, model), BF16),
        gwi_s=((half, units), BF16),
        gwi_r=((half, units), BF16),
        gwi_o=((zrows, units), F32),
        gwi_zs=((4, zrows, units), BF16),
        gwi_zr=((5, zrows, units), BF16),
        gwi_p=((zrows, units), BF16),
        gwi_pr=((4, rows, units), BF16),
        gqk_s=((half, 3 * wid), BF16),
        gqk_r=((half, 3 * wid), BF16),
        gqk_o=((zrows, 3 * wid), F32),
        gqk_zs=((4, zrows, 3 * wid), BF16),
        gqk_zr=((5, zrows, 3 * wid), BF16),
        gqk_p=((zrows, 3 * wid), BF16),
        gqk_pr=((4, rows, 3 * wid), BF16),
        gwo_s=((half, model), BF16),
        gwo_r=((half, model), BF16),
        gwo_o=((half, model), F32),
        gwo_p=((half, model), BF16),
        gwo_pr=((4, PLANES, rows, model), BF16),
        gwo_t=((rows, model), F32),
        gwo_zs=((4, rows, model), BF16),
        gwo_zr=((5, rows, model), BF16),
        smg=((16, model), F32),
        stq=((PLANE, rows, 3 * wid), BF16),
        sti=((PLANE, rows, units), BF16),
        sma=((8, 16, 128), F32),
        smb=((16, 128), F32),
        smb_r=((4, 16, 128), F32),
    )


N_SEND = 160
N_RECV = 160


def fused(plan, tok, model, hidden, *refs):
    (x_ref, cot_ref, table_ref, small_ref, info_ref, wqkv_ref, wo_ref, win_ref, wfo_ref) = refs[:9]
    (out_ref, ig_ref, dwqkv_ref, dwo_ref, dwin_ref, dwfo_ref, sg_ref) = refs[9:16]
    s = Names()
    for name, ref in zip(plan, refs[16:]):
        setattr(s, name, ref)
    send_pool, recv_pool = refs[16 + len(plan):]

    chunk = 2 * tok
    toks = PLANE * chunk
    keys = 2 * toks
    wid = model // PLANE
    units = hidden // PLANE
    rows = model // 32
    zrows = PLANE * rows
    half = PLANES * zrows
    heads = wid // HEAD
    frows = hidden // 32

    c = lax.axis_index("dp")
    b = lax.axis_index("blk")
    z = b // PLANE
    p = b % PLANE
    y, x = p // 2, p % 2
    other = 1 - c
    plane_peers = [p, y * 2 + (1 - x), (1 - y) * 2 + x, PLANE - 1 - p]
    z_peers = [(z + k) % PLANES for k in range(PLANES)]
    z_back = [(z + PLANES - k) % PLANES for k in range(PLANES)]

    def dev(cc, zz, pp):
        return {"dp": cc, "blk": zz * PLANE + pp}

    used = ({}, {})

    def sem(kind, name):
        table = used[kind]
        if name not in table:
            table[name] = len(table)
            assert table[name] < (N_SEND, N_RECV)[kind]
        return (send_pool, recv_pool)[kind].at[table[name]]

    pending = []

    def remote(src, dst, send_name, recv_name, target):
        pltpu.make_async_remote_copy(
            src_ref=src,
            dst_ref=dst,
            send_sem=sem(SEND, send_name),
            recv_sem=sem(RECV, recv_name),
            device_id=target,
            device_id_type=MESH,
        ).start()

    def sent(ref, send_name, cond=None):
        pending.append((ref, send_name, cond))

    def flush_sent():
        for ref, send_name, cond in pending:
            def one():
                handle = sem(SEND, send_name)
                pltpu.make_async_copy(ref, ref, handle).wait()
            if cond is None:
                one()
            else:
                pl.when(cond)(one)
        pending.clear()

    def arrived(ref, recv_name):
        pltpu.make_async_copy(ref, ref, sem(RECV, recv_name)).wait()

    def maybe_local(src, dst, send_name, recv_name, target, is_self):
        send_handle = sem(SEND, send_name)
        recv_handle = sem(RECV, recv_name)

        @pl.when(is_self)
        def _():
            pltpu.make_async_copy(src, dst, recv_handle).start()

        @pl.when(jnp.logical_not(is_self))
        def _():
            pltpu.make_async_remote_copy(
                src_ref=src, dst_ref=dst, send_sem=send_handle, recv_sem=recv_handle,
                device_id=target, device_id_type=MESH,
            ).start()

        sent(src, send_name, jnp.logical_not(is_self))

    outer = z % 3 == 0
    inner = jnp.logical_not(outer)
    o_near, o_far, o_other = 1 + z // 3, 2 - z // 3, 3 - z
    i_near, i_far, i_pair = 3 * (z - 1), 6 - 3 * z, 3 - z

    class ZGather:
        def __init__(self, name, block, half_ref, src=None, sibling=True):
            self.name, self.block, self.src, self.sibling = name, block, src, sibling
            one = block(0)
            sent(one, (name, N.o), outer)
            for key in (N.i0, N.f0, N.i1, N.f1, N.f2):
                sent(one, (name, key), inner)
            if sibling:
                sent(half_ref, (name, N.s))
            self.half_ref = half_ref

        def send(self, zz, key, target, src=None):
            ref = self.block(zz)
            remote(ref if src is None else src, ref, (self.name, key), (self.name, key), dev(c, target, p))

        def over(self, zz, src=None):
            if self.sibling:
                ref = self.block(zz)
                remote(ref if src is None else src, ref, (self.name, N.s), (self.name, N.s), dev(other, z, p))

        def take(self, zz, key):
            arrived(self.block(zz), (self.name, key))

        def step0(self):
            @pl.when(outer)
            def _():
                self.send(z, N.o, o_near, self.src)

            @pl.when(inner)
            def _():
                self.send(z, N.i0, i_pair, self.src)
                self.send(z, N.f0, i_near, self.src)

            self.over(z, self.src)

        def step1(self):
            @pl.when(inner)
            def _():
                self.take(i_near, N.o)
                self.send(i_near, N.i1, i_pair)
                self.take(i_pair, N.i0)
                self.send(i_pair, N.f1, i_near)
                self.over(i_near)
                self.over(i_pair)

            @pl.when(outer)
            def _():
                self.take(o_near, N.f0)
                self.over(o_near)

        def step2(self):
            @pl.when(inner)
            def _():
                self.take(i_far, N.i1)
                self.send(i_far, N.f2, i_near)
                self.over(i_far)

            @pl.when(outer)
            def _():
                self.take(o_far, N.f1)
                self.over(o_far)

        def step3(self):
            @pl.when(outer)
            def _():
                self.take(o_other, N.f2)
                self.over(o_other)

        def done(self):
            arrived(self.half_ref, (self.name, N.s))

    class ZScatter:
        def __init__(self, name, part, keep, got):
            self.name, self.part, self.keep, self.got = name, part, keep, got
            for key in (N.o0, N.o1, N.o2):
                sent(part.at[0], (name, key), outer)
            for key in (N.i0, N.i1, N.f):
                sent(part.at[0], (name, key), inner)

        def put(self, zz, value):
            mine_block = zz == z

            @pl.when(mine_block)
            def _():
                self.keep[...] = value

            @pl.when(jnp.logical_not(mine_block))
            def _():
                self.part[zz] = value.astype(BF16)

        def send(self, zz, slot_id, key, target):
            remote(self.part.at[zz], self.got.at[slot_id], (self.name, key), (self.name, key), dev(c, target, p))

        def take(self, slot_id, key):
            arrived(self.got.at[slot_id], (self.name, key))
            return self.got[slot_id].astype(F32)

        def grow(self, zz, more):
            self.part[zz] = (self.part[zz].astype(F32) + more).astype(BF16)

        def start(self, j):
            if j == 3:
                return

            @pl.when(outer)
            def _():
                self.send((o_other, o_far, o_near)[j], j, (N.o0, N.o1, N.o2)[j], o_near)

        def step0(self):
            for j in range(3):
                self.start(j)

        def step1(self):
            @pl.when(inner)
            def _():
                self.grow(i_far, self.take(0, N.o0))
                self.send(i_far, 3, N.i0, i_pair)
                self.grow(i_pair, self.take(1, N.o1))
                self.send(i_pair, 4, N.i1, i_pair)

        def step2(self):
            @pl.when(inner)
            def _():
                self.grow(i_near, self.take(3, N.i0))
                self.send(i_near, 0, N.f, i_near)
                self.keep[...] += self.take(2, N.o2)

        def step3(self):
            @pl.when(inner)
            def _():
                self.keep[...] += self.take(4, N.i1)

            @pl.when(outer)
            def _():
                self.keep[...] += self.take(0, N.f)

    class PlaneGather:
        def __init__(self, name, pieces, sizes):
            self.name, self.pieces, self.sizes = name, pieces, sizes
            for k in (1, 2):
                for h in (0, 1):
                    sent(sizes[h], (name, k, h))
                sent(sizes[2 - k], (name, 3, k))

        def send(self, pp, h, target, key, recv_key):
            for ref in self.pieces(pp, h):
                remote(ref, ref, (self.name,) + key, (self.name,) + recv_key, dev(c, z, target))

        def step0(self):
            for h in (1, 0):
                self.send(p, h, plane_peers[2], (2, h), (2, h))
                self.send(p, 1 - h, plane_peers[1], (1, 1 - h), (1, 1 - h))

        def step1(self):
            arrived(self.sizes[0], (self.name, 1, 0))
            self.send(plane_peers[1], 0, plane_peers[2], (3, 2), (3, 0))
            arrived(self.sizes[1], (self.name, 2, 1))
            self.send(plane_peers[2], 1, plane_peers[1], (3, 1), (3, 1))

        def done(self, k):
            if k in (1, 2):
                arrived(self.sizes[2 - k], (self.name, k, 2 - k))
            if k == 3:
                for h in (0, 1):
                    arrived(self.sizes[h], (self.name, 3, h))

    barrier = pltpu.get_barrier_semaphore()
    greeted = [dev(c, z, plane_peers[k]) for k in (1, 2, 3)]
    greeted += [dev(c, z_peers[k], p) for k in (1, 2, 3)]
    greeted += [dev(other, z_peers[k], p) for k in (0, 1, 2, 3)]
    for target in greeted:
        pl.semaphore_signal(barrier, inc=1, device_id=target, device_id_type=MESH)
    wrow = (c * 16 + z * 4 + p) * rows
    own_w = wide_slice(wrow, rows, rows)
    fblock = (c * 4 + z) * frows
    for pp in range(PLANE):
        for t in range(3):
            s.stq[pp, :, t * wid:(t + 1) * wid] = wqkv_ref[:, t * model + pp * wid:t * model + (pp + 1) * wid]
        for g in range(8):
            source = (g * PLANE + pp) * frows
            s.sti[pp, :, g * frows:(g + 1) * frows] = win_ref[:, source:source + frows]
    s.wqkv[own_w, :] = s.stq[p]
    s.win[own_w, :] = s.sti[p]
    s.wo[own_w, :] = wo_ref[...]
    s.wfo[wide_slice(fblock, frows, frows), :] = wfo_ref[...]
    s.smalls[c, z, p] = small_ref[...]
    pl.semaphore_wait(barrier, len(greeted))

    home = z // 2
    slot = z % 2
    for i in range(2):
        plane_of = 2 * c + i
        is_self = jnp.logical_and(home == c, plane_of == z)
        target = dev(home, plane_of, p)
        maybe_local(x_ref.at[i], s.xin.at[wide_slice(slot * tok, tok, tok)], (N.x, i), N.x, target, is_self)
        maybe_local(info_ref.at[i], s.inf_in.at[slot], (N.i, i), N.i, target, is_self)

    table_here = home == c

    @pl.when(table_here)
    def _():
        remote(table_ref.at[slot], s.tbl, N.tbl, N.tbl, dev(other, z, p))
        s.tbl[...] = table_ref[slot]

    for k in (3, 1, 2):
        pp = plane_peers[k]
        remote(s.stq.at[pp], s.wqkv.at[own_w], (N.wq1, k), (N.wq1, k), dev(c, z, pp))
        sent(s.stq.at[0], (N.wq1, k))
    woz = ZGather(
        N.woz, lambda zz: s.wo.at[wide_slice((c * 16 + zz * 4 + p) * rows, rows, rows)], None, src=wo_ref, sibling=False
    )
    wf = ZGather(
        N.wf, lambda zz: s.wfo.at[wide_slice((c * 4 + zz) * frows, frows, frows)], s.wfo.at[pl.ds(0, 4 * frows)], src=wfo_ref
    )
    for k in (1, 2, 3):
        remote(small_ref, s.smalls.at[c, z, p], N.smz, (N.smz, k), dev(c, z_peers[k], p))
    sent(s.smalls.at[0, 0, pl.ds(0, 3)], N.smz)

    wi = ZGather(
        N.wi, lambda zz: s.win.at[wide_slice(c * half + zz * zrows, zrows, zrows)], s.win.at[pl.ds(0, half)]
    )
    woz.step0()
    for k in (3, 1, 2):
        pp = plane_peers[k]
        remote(s.sti.at[pp], s.win.at[own_w], (N.wi1, k), (N.wi1, k), dev(c, z, pp))
        sent(s.sti.at[0], (N.wi1, k))
    for k in (1, 2, 3):
        arrived(s.stq.at[0], (N.wq1, k))
    wq = ZGather(
        N.wq, lambda zz: s.wqkv.at[wide_slice(c * half + zz * zrows, zrows, zrows)], s.wqkv.at[pl.ds(0, half)]
    )
    wq.step0()

    arrived(s.inf_in, N.i)
    info_own = s.inf_in[0] + s.inf_in[1]
    s.inf[c * 4 + p] = info_own
    for k in (1, 2, 3):
        blk_ref = s.inf.at[c * 4 + p]
        remote(blk_ref, blk_ref, N.inf, (N.inf, k), dev(c, z, plane_peers[k]))
    sent(s.inf.at[pl.ds(0, 3)], N.inf)

    @pl.when(jnp.logical_not(table_here))
    def _():
        arrived(s.tbl, N.tbl)

    arrived(s.xin, N.x)
    items = lax.broadcasted_iota(jnp.int32, (8, chunk), 0).astype(F32)
    onehot = jnp.where(info_own[0:1, :] == items + 1.0, 1.0, 0.0)
    embedded = lax.dot_general(
        onehot, s.tbl[...], (((0,), (0,)), ((), ())), precision=lax.Precision.HIGHEST,
        preferred_element_type=F32,
    )
    start_res = s.xin[...].astype(F32) + embedded
    s.sres[...] = start_res
    prow = p * chunk
    own_rows = wide_slice(prow, chunk, chunk)
    s.slow[own_rows, :] = start_res.astype(BF16)

    def plane_gather(ref, name):
        gather = PlaneGather(
            name,
            lambda pp, h: [ref.at[wide_slice(pp * chunk + h * tok, tok, tok)]],
            (ref.at[pl.ds(0, tok)], ref.at[pl.ds(0, tok)]),
        )
        gather.step0()
        return gather

    slow_gather = plane_gather(s.slow, N.slow)

    for k in (1, 2, 3):
        arrived(s.smalls.at[0, 0, 0], (N.smz, k))
    for k in (1, 2, 3):
        for zz in range(PLANES):
            ref = s.smalls.at[c, zz, p]
            remote(ref, ref, N.smp, (N.smp, k), dev(c, z, plane_peers[k]))
    sent(s.smalls.at[0, pl.ds(0, 3)], N.smp)
    for k in (1, 2, 3):
        arrived(s.inf.at[0], (N.inf, k))
    inf_half = s.inf.at[wide_slice(c * 4, 4, 4)]
    remote(inf_half, inf_half, N.infs, N.infs, dev(other, z, p))
    sent(inf_half, N.infs)
    for k in (1, 2, 3):
        arrived(s.sti.at[0], (N.wi1, k))
    wi.step0()
    slow_gather.step1()
    wq.step1()
    woz.step1()
    for k in (1, 2, 3):
        arrived(s.smalls.at[0, 0], (N.smp, k))
    remote(s.smalls.at[c], s.smalls.at[c], N.sms, N.sms, dev(other, z, p))
    sent(s.smalls.at[0], N.sms)
    wf.step0()
    wq.step2()
    woz.step2()
    arrived(s.smalls.at[0], N.sms)
    pieces = s.smalls[...].reshape(512, 128)
    lane = lax.broadcasted_iota(jnp.int32, (128, model), 1)
    sub = lax.broadcasted_iota(jnp.int32, (128, model), 0)
    spread = jnp.where(lane % rows == sub, 1.0, 0.0).astype(BF16)
    laid = mm(pieces, spread)
    lane2 = lax.broadcasted_iota(jnp.int32, (512, model), 1)
    sub2 = lax.broadcasted_iota(jnp.int32, (512, model), 0)
    laid = jnp.where(lane2 // rows == sub2 // 16, laid, 0.0)
    s.vec[...] = jnp.sum(laid.reshape(32, 16, model), axis=0)
    for g in range(8):
        s.ffb[:, pl.ds(g * frows, frows)] = s.smalls[g // 4, g % 4, p].astype(F32)
    arrived(inf_half, N.infs)
    code_hot = []
    for g in range(8):
        code_hot.append(jnp.where(s.inf[g][1:2, :] == items + 1.0, 1.0, 0.0))
    seg_hot = []
    for g in range(4):
        seg_hot.append(jnp.where(s.inf[c * 4 + g][0:1, :] == items + 1.0, 1.0, 0.0))
    code_hot = jnp.concatenate(code_hot, axis=1)
    seg_hot = jnp.concatenate(seg_hot, axis=1)
    s.bias[...] = (mm(seg_hot, code_hot, 0, 0) - 1.0) * -NEGATIVE

    wq.step3()
    wq.done()

    q_bias = s.vec[0:1, wide_slice(p * wid, wid, wid)]
    v_bias = s.vec[1:2, wide_slice(p * wid, wid, wid)]
    for k in range(4):
        pp = plane_peers[k]
        here = wide_slice(pp * chunk, chunk, chunk)
        slow_gather.done(k)
        low_chunk = s.slow[here, :]
        krow = wide_slice(c * toks + pp * chunk, chunk, chunk)
        s.kv[krow, 0:wid] = mm(low_chunk, s.wqkv[:, wid:2 * wid]).astype(BF16)
        s.kv[krow, wid:2 * wid] = (mm(low_chunk, s.wqkv[:, 2 * wid:3 * wid]) + v_bias).astype(BF16)
        remote(s.kv.at[krow], s.kv.at[krow], N.kv, N.kv, dev(other, z, p))
        s.q[here, :] = (mm(low_chunk, s.wqkv[:, 0:wid]) + q_bias).astype(BF16)
    kv_half = s.kv.at[wide_slice(c * toks, toks, toks)]
    sent(kv_half, N.kv)

    woz.step3()
    wop = PlaneGather(
        N.wop,
        lambda pp, h: [
            s.wo.at[wide_slice((c * 16 + (2 * h + g) * 4 + pp) * rows, rows, rows)] for g in range(2)
        ],
        (s.wo.at[pl.ds(0, 2 * rows)], s.wo.at[pl.ds(0, 2 * rows)]),
    )
    wop.step0()
    wi.step1()
    arrived(kv_half, N.kv)

    scale = HEAD ** (-0.5)
    qt = TILE
    s.att[...] = jnp.zeros_like(s.att)

    def head_mask(h, n):
        return lax.broadcasted_iota(jnp.int32, (n, wid), 1) // HEAD == h

    def attend(step, carry):
        h = step % heads
        t = step // heads
        here = wide_slice(t * qt, qt, qt)
        mask = head_mask(h, qt)
        queries = jnp.where(mask, s.q[here, :].astype(F32) * scale, 0.0).astype(BF16)
        scores = mm(queries, s.kv[:, 0:wid], 1, 1) + s.bias[here, :]
        top = jnp.max(scores, axis=-1, keepdims=True)
        weights = jnp.exp(scores - top)
        total = jnp.sum(weights, axis=-1, keepdims=True)
        result = mm(weights.astype(BF16), s.kv[:, wid:2 * wid]) / total
        s.att[here, :] = jnp.where(mask, result, s.att[here, :])
        s.lse[h, here, :] = top + jnp.log(total)
        return carry

    steps = heads * (toks // qt)
    lax.fori_loop(0, steps // 4, attend, 0)
    wf.step1()
    lax.fori_loop(steps // 4, steps // 2, attend, 0)
    wop.step1()
    lax.fori_loop(steps // 2, steps, attend, 0)
    s.attl[...] = s.att[...].astype(BF16)
    for k in (1, 2, 3):
        pp = plane_peers[k]
        remote(
            s.attl.at[wide_slice(pp * chunk, chunk, chunk)],
            s.attx.at[:, wide_slice(p * wid, wid, wid)],
            N.attx, (N.attx, k), dev(c, z, pp),
        )
    sent(s.attl.at[pl.ds(0, 3 * chunk)], N.attx)
    s.attx[:, wide_slice(p * wid, wid, wid)] = s.attl[own_rows, :]

    for k in (1, 2, 3):
        wop.done(k)
    wo_half = s.wo.at[wide_slice(c * half, half, half)]
    remote(wo_half, wo_half, N.wos, N.wos, dev(other, z, p))
    sent(wo_half, N.wos)
    arrived(s.wo.at[pl.ds(0, half)], N.wos)
    for k in (1, 2, 3):
        arrived(s.attl.at[pl.ds(0, chunk)], (N.attx, k))

    def row_vec(r):
        return s.vec[r:r + 1, :]

    def normalize_rows(hidden_rows):
        centered = hidden_rows - jnp.mean(hidden_rows, axis=-1, keepdims=True)
        inverse = lax.rsqrt(jnp.mean(centered * centered, axis=-1, keepdims=True) + EPSILON)
        return centered * inverse, inverse

    branch = mm(s.attx[...], s.wo[...]) + row_vec(2)
    normed, inverse = normalize_rows(s.sres[...] + branch)
    after = normed * row_vec(3) + row_vec(4)
    s.hid[own_rows, :] = after.astype(BF16)
    hid_gather = plane_gather(s.hid, N.hid)
    s.n1[...] = normed
    s.inv1[...] = inverse
    s.aft[...] = after
    wi.step2()
    wf.step2()
    for i in range(2):
        plane_of = 2 * c + i
        is_self = jnp.logical_and(home == c, plane_of == z)
        target = dev(home, plane_of, p)
        maybe_local(cot_ref.at[i], s.cin.at[wide_slice(slot * tok, tok, tok)], (N.c, i), N.c, target, is_self)

    wi.step3()
    wi.done()

    def ffn_first(here):
        def one(n, carry):
            cols = wide_slice(n * TILE, TILE, TILE)
            acc = mm(s.hid[here, :], s.win[:, cols]) + s.ffb[8:9, cols]
            phi = 0.5 * (1.0 + lax.erf(acc * (2.0 ** -0.5)))
            s.act[here, cols] = (acc * phi).astype(BF16)
            s.pre[here, cols] = phi + acc * jnp.exp(-0.5 * acc * acc) * (1.0 / math.sqrt(2.0 * math.pi))
            return carry
        lax.fori_loop(0, units // TILE, one, 0, unroll=True)

    def column_tiles(fn, total, dst, dst_rows=None):
        def one(n, carry):
            cols = wide_slice(n * TILE, TILE, TILE)
            value = fn(cols).astype(dst.dtype)
            if dst_rows is None:
                dst[:, cols] = value
            else:
                dst[dst_rows, cols] = value
            return carry
        lax.fori_loop(0, total // TILE, one, 0, unroll=True)

    top_half, low_half = pl.ds(0, tok), pl.ds(tok, tok)
    rs_keys = ((1, 0), (1, 1), (2, 0), (2, 1), (3, 0), (3, 1))

    def scatter_send(name, k, h, dst, target):
        rows_of = (top_half, low_half)[h]
        remote(s.fs.at[k, rows_of], dst.at[rows_of], (name, k, h), (name, k, h), dev(c, z, plane_peers[target]))

    def plane_scatter_chunk(k, fn, name):
        if k == 0:
            column_tiles(fn, model, s.own)
            return
        column_tiles(fn, model, s.fs.at[k])
        scatter_start(k, name)

    def scatter_start(k, name):
        if k == 1:
            scatter_send(name, 1, 0, s.fr.at[1], 1)
        if k == 2:
            scatter_send(name, 2, 1, s.fr.at[2], 2)
        if k == 3:
            scatter_send(name, 3, 0, s.fr.at[0], 1)
            scatter_send(name, 3, 1, s.fr.at[0], 2)

    def plane_scatter_pass(name):
        for h, k in ((0, 2), (1, 1)):
            rows_of = (top_half, low_half)[h]
            arrived(s.fr.at[0, rows_of], (name, 3, h))
            s.fs[k, rows_of, :] = (
                s.fs[k, rows_of, :].astype(F32) + s.fr[0, rows_of, :].astype(F32)
            ).astype(BF16)
            scatter_send(name, k, h, s.fr.at[k], k)

    def plane_scatter_sum(name):
        for k in (1, 2):
            for h in (0, 1):
                arrived(s.fr.at[k, top_half], (name, k, h))
        return s.own[...] + s.fr[1].astype(F32) + s.fr[2].astype(F32)

    def plane_sent_now(name):
        for k, h in rs_keys:
            ref = s.fs.at[k, top_half]
            pltpu.make_async_copy(ref, ref, sem(SEND, (name, k, h))).wait()

    def chunk_rows(k):
        return wide_slice(plane_peers[k] * chunk, chunk, chunk)

    for k in range(4):
        here = chunk_rows(k)
        hid_gather.done(k)
        ffn_first(here)
        if k == 0:
            hid_gather.step1()
    wf.step3()
    wf.done()
    for k in (3, 1, 2, 0):
        here = chunk_rows(k)
        plane_scatter_chunk(k, lambda cols: mm(s.act[here, :], s.wfo[:, cols]), N.rs1)
    plane_scatter_pass(N.rs1)

    branch = plane_scatter_sum(N.rs1) + row_vec(5)
    normed2, inverse2 = normalize_rows(s.aft[...] + branch)
    gain2 = row_vec(6)
    arrived(s.cin, N.c)
    upstream = s.cin[...].astype(F32)

    def norm_back(up, normed_rows, inverse_rows, gain):
        scaled = up * gain
        return inverse_rows * (
            scaled
            - jnp.mean(scaled, axis=-1, keepdims=True)
            - normed_rows * jnp.mean(scaled * normed_rows, axis=-1, keepdims=True)
        )

    second = norm_back(upstream, normed2, inverse2, gain2)
    second_low = second.astype(BF16)
    s.bg[own_rows, :] = second_low
    bg_gather = plane_gather(s.bg, N.bg)
    s.second[...] = second
    s.outl[...] = (normed2 * gain2 + row_vec(7)).astype(BF16)
    s.smg[...] = jnp.zeros_like(s.smg)
    s.smg[6:7, :] = jnp.sum(upstream * normed2, axis=0, keepdims=True)
    s.smg[7:8, :] = jnp.sum(upstream, axis=0, keepdims=True)
    s.smg[5:6, :] = jnp.sum(second_low.astype(F32), axis=0, keepdims=True)

    def send_home(src, dst, name):
        for i in range(2):
            is_self = jnp.logical_and(home == c, 2 * c + i == z)
            maybe_local(
                src.at[pl.ds(i * tok, tok)], dst.at[slot], (name, i), name,
                dev(home, 2 * c + i, p), is_self,
            )

    send_home(s.outl, s.outr, N.out)

    def ffn_back(here):
        def one(n, carry):
            cols = wide_slice(n * TILE, TILE, TILE)
            acc = mm(s.bg[here, :], s.wfo[cols, :], 1, 1)
            s.pg[here, cols] = (acc * s.pre[here, cols]).astype(BF16)
            return carry
        lax.fori_loop(0, units // TILE, one, 0, unroll=True)

    def turn(j):
        return (z // 2) * (2 * j - 3) + 3 - j

    def grad_sibling(lhs, rhs, buf_s, buf_r, name):
        for j in range(4):
            at = wide_slice(turn(j) * zrows, zrows, zrows)
            cols = wide_slice(other * half + turn(j) * zrows, zrows, zrows)
            buf_s[at, :] = mm(lhs[:, cols], rhs[...], 0, 0).astype(BF16)
            remote(buf_s.at[at], buf_r.at[at], (name, j), (name, j), dev(other, z, p))
            sent(buf_s.at[pl.ds(0, zrows)], (name, j))

    def sibling_send(buf_s, buf_r, name):
        remote(buf_s, buf_r, name, name, dev(other, z, p))
        sent(buf_s, name)

    def grad_own(lhs, rhs, buf_r, scatter, name):
        for j in range(4):
            at = wide_slice(turn(j) * zrows, zrows, zrows)
            cols = wide_slice(c * half + turn(j) * zrows, zrows, zrows)
            arrived(buf_r.at[pl.ds(0, zrows)], (name, j))
            scatter.put(turn(j), mm(lhs[:, cols], rhs[...], 0, 0) + buf_r[at, :].astype(F32))
            scatter.start(j)

    gfo = ZScatter((N.gfo, N.z), s.gfo_zs, s.gfo_o, s.gfo_zr)
    gwi = ZScatter((N.gwi, N.z), s.gwi_zs, s.gwi_o, s.gwi_zr)
    gqk = ZScatter((N.gqk, N.z), s.gqk_zs, s.gqk_o, s.gqk_zr)
    gwo = ZScatter((N.gwo, N.z), s.gwo_zs, s.gwo_t, s.gwo_zr)

    plane_sent_now(N.rs1)

    def hidden_chunk(k):
        here = chunk_rows(k)
        plane_scatter_chunk(k, lambda cols: mm(s.pg[here, :], s.win[cols, :], 1, 1), N.rs2)

    for k in range(4):
        bg_gather.done(k)
        if k == 3:
            grad_sibling(s.act, s.bg, s.gfo_s, s.gfo_r, N.gfo)
        ffn_back(chunk_rows(k))
        if k == 3:
            grad_own(s.act, s.bg, s.gfo_r, gfo, N.gfo)
        if k == 0:
            bg_gather.step1()
        else:
            hidden_chunk(k)
    plane_scatter_pass(N.rs2)
    grad_sibling(s.hid, s.pg, s.gwi_s, s.gwi_r, N.gwi)
    hidden_chunk(0)
    s.smg[8:9, :] = jnp.sum(s.pg[...].astype(F32), axis=0, keepdims=True)
    grad_own(s.hid, s.pg, s.gwi_r, gwi, N.gwi)

    hidden_grad = s.second[...] + plane_scatter_sum(N.rs2)
    normed = s.n1[...]
    first = norm_back(hidden_grad, normed, s.inv1[...], row_vec(3))
    first_low = first.astype(BF16)
    s.agl[...] = first_low
    for k in (3, 1, 2, 0):
        pp = plane_peers[k]
        cols = wide_slice(pp * wid, wid, wid)
        s.ado[:, cols] = mm(first_low, s.wo[cols, :], 1, 1).astype(BF16)
        if k:
            remote(s.ado.at[:, cols], s.do.at[own_rows], N.do, (N.do, k), dev(c, z, pp))
    sent(s.do.at[pl.ds(0, 3 * chunk)], N.do)
    s.first[...] = first
    s.smg[3:4, :] = jnp.sum(hidden_grad * normed, axis=0, keepdims=True)
    s.smg[4:5, :] = jnp.sum(hidden_grad, axis=0, keepdims=True)
    s.smg[2:3, :] = jnp.sum(first_low.astype(F32), axis=0, keepdims=True)
    s.do[own_rows, :] = s.ado[:, wide_slice(p * wid, wid, wid)]

    grad_sibling(s.attx, s.agl, s.gwo_s, s.gwo_r, N.gwo)

    for k in (1, 2, 3):
        arrived(s.do.at[pl.ds(0, chunk)], (N.do, k))

    s.dq[...] = jnp.zeros_like(s.dq)
    s.dk[...] = jnp.zeros_like(s.dk)
    s.dv[...] = jnp.zeros_like(s.dv)

    def attend_back(step, carry):
        h = step % heads
        t = step // heads
        here = wide_slice(t * qt, qt, qt)
        mask = head_mask(h, qt)
        queries = jnp.where(mask, s.q[here, :].astype(F32) * scale, 0.0).astype(BF16)
        scores = mm(queries, s.kv[:, 0:wid], 1, 1) + s.bias[here, :]
        probs = jnp.exp(scores - s.lse[h, here, :])
        grads = jnp.where(mask, s.do[here, :].astype(F32), 0.0)
        residue = jnp.sum(grads * s.att[here, :], axis=-1, keepdims=True)
        grads = grads.astype(BF16)
        prob_grad = mm(grads, s.kv[:, wid:2 * wid], 1, 1)
        score_grad = (probs * (prob_grad - residue)).astype(BF16)
        s.dv[...] += mm(probs.astype(BF16), grads, 0, 0)
        s.dk[...] += mm(score_grad, queries, 0, 0)
        s.dq[here, :] += jnp.where(mask, mm(score_grad, s.kv[:, 0:wid]), 0.0)
        return carry

    lax.fori_loop(0, steps // 4, attend_back, 0)
    for j in range(4):
        arrived(s.gwo_r.at[pl.ds(0, zrows)], (N.gwo, j))

    def own_tile(m, carry):
        at = wide_slice(m * TILE, TILE, TILE)
        cols = wide_slice(c * half + m * TILE, TILE, TILE)
        value = mm(s.attx[:, cols], s.agl[...], 0, 0) + s.gwo_r[at, :].astype(F32)
        s.gwo_o[at, :] = value
        s.gwo_p[at, :] = value.astype(BF16)
        return carry

    lax.fori_loop(0, half // TILE, own_tile, 0)

    for k in (1, 2, 3):
        for zz in range(PLANES):
            remote(
                s.gwo_p.at[wide_slice(zz * zrows + plane_peers[k] * rows, rows, rows)],
                s.gwo_pr.at[k, zz],
                N.gwop, (N.gwop, k), dev(c, z, plane_peers[k]),
            )
    sent(s.gwo_p.at[pl.ds(0, 3 * PLANES * rows)], N.gwop)
    gfo.step1()
    lax.fori_loop(steps // 4, steps // 2, attend_back, 0)
    lax.fori_loop(steps // 2, 3 * steps // 4, attend_back, 0)
    gfo.step2()
    lax.fori_loop(3 * steps // 4, steps, attend_back, 0)
    gwi.step1()
    theirs = wide_slice(other * toks, toks, toks)
    mine = wide_slice(c * toks, toks, toks)
    s.dkvs[:, 0:wid] = s.dk[theirs, :].astype(BF16)
    s.dkvs[:, wid:2 * wid] = s.dv[theirs, :].astype(BF16)
    sibling_send(s.dkvs, s.dkvr, N.dkv)
    s.dqkv[:, 0:wid] = (s.dq[...] * scale).astype(BF16)

    for k in (1, 2, 3):
        arrived(s.gwo_pr.at[k], (N.gwop, k))

    def gwo_total(zz):
        value = s.gwo_o[wide_slice(zz * zrows + p * rows, rows, rows), :]
        for k in (1, 2, 3):
            value = value + s.gwo_pr[k, zz].astype(F32)
        return value

    for k in (2, 3, 1):
        s.gwo_zs[z_peers[k]] = gwo_total(z_peers[k]).astype(BF16)
    s.gwo_t[...] = gwo_total(z)
    gwo.step0()

    arrived(s.dkvr, N.dkv)
    s.dqkv[:, wid:2 * wid] = (s.dk[mine, :] + s.dkvr[:, 0:wid].astype(F32)).astype(BF16)
    s.dqkv[:, 2 * wid:3 * wid] = (s.dv[mine, :] + s.dkvr[:, wid:2 * wid].astype(F32)).astype(BF16)

    plane_sent_now(N.rs2)
    for k in (3, 1, 2, 0):
        here = chunk_rows(k)
        plane_scatter_chunk(k, lambda cols: mm(s.dqkv[here, :], s.wqkv[cols, :], 1, 1), N.rs3)

    grad_sibling(s.slow, s.dqkv, s.gqk_s, s.gqk_r, N.gqk)
    plane_scatter_pass(N.rs3)
    grad_own(s.slow, s.dqkv, s.gqk_r, gqk, N.gqk)
    gwi.step2()
    gwo.step1()

    low_sum = jnp.sum(s.dqkv[...].astype(F32), axis=0, keepdims=True)
    pcols = wide_slice(p * wid, wid, wid)
    s.smg[0:1, pcols] = low_sum[:, 0:wid]
    s.smg[1:2, pcols] = low_sum[:, 2 * wid:3 * wid]
    for cc in range(2):
        for k in range(4):
            if cc == 0 and k == 0:
                continue
            tc = other if cc else c
            lanes = wide_slice((tc * 4 + z_peers[k]) * 128, 128, 128)
            remote(s.smg.at[:, lanes], s.sma.at[cc * 4 + k], N.sma, (N.sma, cc, k), dev(tc, z_peers[k], p))
    sent(s.smg.at[:, pl.ds(0, 7 * 128)], N.sma)
    gwo.step2()

    total = s.first[...] + plane_scatter_sum(N.rs3)
    s.igl[...] = total.astype(BF16)
    send_home(s.igl, s.igr, N.ig)

    gwi.step3()

    def plane_rows(buf_p, buf_pr, name):
        for k in (1, 2, 3):
            remote(
                buf_p.at[wide_slice(plane_peers[k] * rows, rows, rows)], buf_pr.at[k],
                name, (name, k), dev(c, z, plane_peers[k]),
            )
        sent(buf_p.at[pl.ds(0, 3 * rows)], name)

    s.gwi_p[...] = s.gwi_o[...].astype(BF16)
    plane_rows(s.gwi_p, s.gwi_pr, N.gwip)
    gqk.step1()
    gfo.step3()
    dwfo_ref[...] = s.gfo_o[...]

    def dwin_piece(k):
        if k:
            arrived(s.gwi_pr.at[k], (N.gwip, k))
        pp = plane_peers[k]
        for g in range(8):
            piece_cols = slice(g * frows, (g + 1) * frows)
            if k:
                value = s.gwi_pr[k, :, piece_cols].astype(F32)
            else:
                value = s.gwi_o[wide_slice(p * rows, rows, rows), piece_cols]
            dwin_ref[:, wide_slice(g * 4 * frows + pp * frows, frows, frows)] = value

    part = s.smg[:, wide_slice((c * 4 + z) * 128, 128, 128)]
    for cc in range(2):
        for k in range(4):
            if cc == 0 and k == 0:
                continue
            arrived(s.sma.at[cc * 4 + k], (N.sma, cc, k))
            part = part + s.sma[cc * 4 + k]
    s.smb[...] = part
    for k in (1, 2, 3):
        remote(s.smb, s.smb_r.at[k], N.smb, (N.smb, k), dev(c, z, plane_peers[k]))
    sent(s.smb_r.at[pl.ds(0, 3)], N.smb)
    gqk.step2()

    arrived(s.outr, N.out)
    out_ref[...] = s.outr[...]
    for k in range(4):
        dwin_piece(k)
    gqk.step3()
    s.gqk_p[...] = s.gqk_o[...].astype(BF16)
    plane_rows(s.gqk_p, s.gqk_pr, N.gqkp)

    gwo.step3()
    dwo_ref[...] = s.gwo_t[...]
    all_rows = s.smb[...]
    for k in (1, 2, 3):
        arrived(s.smb_r.at[k], (N.smb, k))
        all_rows = all_rows + s.smb_r[k]
    row_ids = lax.broadcasted_iota(jnp.int32, (16, 128), 0)
    sg_ref[...] = jnp.where(row_ids == 8, s.smb[...], all_rows)
    for k in range(4):
        if k:
            arrived(s.gqk_pr.at[k], (N.gqkp, k))
        pp = plane_peers[k]
        for t in range(3):
            piece_cols = slice(t * wid, (t + 1) * wid)
            if k:
                value = s.gqk_pr[k, :, piece_cols].astype(F32)
            else:
                value = s.gqk_o[wide_slice(p * rows, rows, rows), piece_cols]
            dwqkv_ref[:, wide_slice(t * model + pp * wid, wid, wid)] = value
    arrived(s.igr, N.ig)
    ig_ref[...] = s.igr[...]

    @pl.when(table_here)
    def _():
        handle = sem(SEND, N.tbl)
        pltpu.make_async_copy(s.tbl, s.tbl, handle).wait()

    plane_sent_now(N.rs3)
    flush_sent()


def fused_local(
    inputs, segments, pad_mask, timesteps, w_qkv, bias_query, bias_value, w_attn_out, bias_attn_out,
    ln1_gain, ln1_shift, w_ffn_in, bias_ffn_in, w_ffn_out, bias_ffn_out, ln2_gain, ln2_shift, cotangent,
):
    _, tok, model = inputs.shape
    hidden = w_ffn_in.shape[1]
    rows = w_qkv.shape[0]
    blk = lax.axis_index("blk")
    half_width = model // 2
    frequency = jnp.exp(
        jnp.arange(half_width, dtype=F32) * (-math.log(10000.0) / half_width)
    )
    angles = timesteps.astype(F32)[..., None] * (100.0 / TSTEPS) * frequency
    table = jnp.concatenate([jnp.sin(angles), jnp.cos(angles)], axis=-1)
    vectors = jnp.stack(
        [bias_query, bias_value, bias_attn_out, ln1_gain, ln1_shift, bias_ffn_out, ln2_gain, ln2_shift]
    )
    small = jnp.concatenate(
        [
            jnp.pad(vectors, ((0, 0), (0, 128 - rows))),
            bias_ffn_in[None],
            jnp.zeros((7, 128), BF16),
        ]
    )
    codes = jnp.where(pad_mask == 1, segments, -1)
    marks = jnp.stack([segments, codes], axis=1).astype(F32) + 1.0
    odd = (blk // PLANE) % 2 == 1
    marks = jnp.concatenate([jnp.where(odd, 0.0, marks), jnp.where(odd, marks, 0.0)], axis=-1)
    info = jnp.pad(marks, ((0, 0), (0, 6), (0, 0)))

    plan = scratch_plan(tok, model, hidden)
    vmem = pl.BlockSpec(memory_space=pltpu.VMEM)
    outs = pl.pallas_call(
        functools.partial(fused, plan, tok, model, hidden),
        out_shape=(
            jax.ShapeDtypeStruct((2, tok, model), BF16),
            jax.ShapeDtypeStruct((2, tok, model), BF16),
            jax.ShapeDtypeStruct((rows, 3 * model), F32),
            jax.ShapeDtypeStruct((rows, model), F32),
            jax.ShapeDtypeStruct((rows, hidden), F32),
            jax.ShapeDtypeStruct((hidden // 32, model), F32),
            jax.ShapeDtypeStruct((16, 128), F32),
        ),
        in_specs=[vmem] * 9,
        out_specs=[vmem] * 7,
        scratch_shapes=[pltpu.VMEM(shape, dtype) for shape, dtype in plan.values()]
        + [pltpu.SemaphoreType.DMA((N_SEND,)), pltpu.SemaphoreType.DMA((N_RECV,))],
        compiler_params=pltpu.CompilerParams(
            collective_id=0, has_side_effects=True, vmem_limit_bytes=63 * 1024 * 1024
        ),
    )(inputs, cotangent, table, small, info, w_qkv, w_attn_out, w_ffn_in, w_ffn_out)
    out, input_grad, g_qkv, g_out, g_in, g_down, g_small = outs
    mine = lax.dynamic_slice(g_small, (0, (blk % PLANE) * rows), (8, rows))
    return (
        out, input_grad, g_qkv, mine[0], mine[1], g_out, mine[2], mine[3], mine[4],
        g_in, g_small[8], g_down, mine[5], mine[6], mine[7],
    )


def layer(*args):
    inputs, w_qkv, w_ffn_out = args[0], args[4], args[13]
    fits = (
        lax.axis_size("dp") == 2
        and lax.axis_size("blk") == PLANE * PLANES
        and inputs.shape[0] == 2
        and inputs.shape[1] == 64
        and w_qkv.shape[0] * PLANE == 128
        and w_ffn_out.shape[0] == 128
        and args[3].shape[1] <= 8
    )
    return (fused_local if fits else local)(*args)


def solution(mesh):
    return jax.shard_map(
        layer,
        mesh=mesh,
        in_specs=(
            P("dp", "blk", None),
            P("dp", "blk"),
            P("dp", "blk"),
            P("dp", None),
            P(("dp", "blk"), None),
            P(("dp", "blk")),
            P(("dp", "blk")),
            P(("dp", "blk"), None),
            P(("dp", "blk")),
            P(("dp", "blk")),
            P(("dp", "blk")),
            P(("dp", "blk"), None),
            P(("dp", "blk")),
            P(("dp", "blk"), None),
            P(("dp", "blk")),
            P(("dp", "blk")),
            P(("dp", "blk")),
            P("dp", "blk", None),
        ),
        out_specs=(
            P("dp", "blk", None),
            P("dp", "blk", None),
            P(("dp", "blk"), None),
            P(("dp", "blk")),
            P(("dp", "blk")),
            P(("dp", "blk"), None),
            P(("dp", "blk")),
            P(("dp", "blk")),
            P(("dp", "blk")),
            P(("dp", "blk"), None),
            P(("dp", "blk")),
            P(("dp", "blk"), None),
            P(("dp", "blk")),
            P(("dp", "blk")),
            P(("dp", "blk")),
        ),
        check_vma=False,
    )
```
